32 devices in a mesh: seq: 8 (over z, core), chan: 4 (over y, x).
Axes of the slice: x: 2, y: 2, z: 4, core: 2. Of those that a mesh axis runs over, the one named last changes fastest.
Arguments:
- arrived: bfloat16 [3, 4096, 8192], P(None, ('seq', 'chan')), may hold values from -6 to 6
- landing: int32 [8, 8], P('seq'), may hold values from 0 to 7, each once within a row
- resets: int32 [4096], P('seq'), may hold values 0 or 1
- short_taps: float32 [3, 7, 8192], P(None, None, 'chan'), may hold values from -3 to 3
- decay_rate: float32 [16, 8192], P(None, 'chan'), may hold values from 0 to 1, as said below
- residues: float32 [16, 8192], P(None, 'chan'), may hold values from -2 to 2
- skip_gain: float32 [8192], P('chan'), may hold values from 0.5 to 1.5
Outputs:
- mixed: bfloat16 [4096, 8192], P('seq', 'chan')
The draws below stay inside these ranges and needn't reach their ends.
Inputs may be any that keep to these rules, and one draw needn't show every extreme that they name: Each row is a permutation: landing[r, s] is the place, among the blocks of shard r, of the block that comes from loader group s. `resets`: 1 marks the first token of a document. `decay_rate`: positive decay rates.
All inputs are finite; a program needn't handle non-finite values. No bound on the sum of `resets` on one device may be relied on, other than what follows from the above.
Results may differ from the reference program's by a relative error of at most 0.01.
Values may be sent and summed in bfloat16 or wider, within the bound.
No kernel may reach another device: no remote copies, remote signals or barrier semaphores. Data moves between devices by JAX's collectives and lax.ppermute only.
A program may use at most 128 MiB of HBM per device.

```python
import jax
import jax.numpy as jnp
from jax import lax

D = 8192
ORDER = 16
SHORT = 7
TOK_DEV = 512
TOKENS = 4096
SLAB = 64
N_SEQ = 8


def draw_decay_rate(key, part):
    key_spread = jax.random.fold_in(key, 0)
    lowest = jnp.log(jnp.float32(150.0 / (TOKENS * TOKENS)))
    highest = jnp.log(jnp.float32(1.0 / 30.0))
    spread = jax.random.uniform(key_spread, (ORDER, D), jnp.float32)
    log_rates = lowest + spread * (highest - lowest)
    return jnp.exp(log_rates).astype(jnp.float32)


def set_ends(drawn, key, low, largest):
    place = [jax.random.randint(jax.random.fold_in(key, axis), (), 0, length) for axis, length in enumerate(drawn.shape)]
    longest = drawn.shape.index(max(drawn.shape))
    next_to = place[:longest] + [(place[longest] + 1) % drawn.shape[longest]] + place[longest + 1:]
    return drawn.at[tuple(place)].set(low).at[tuple(next_to)].set(largest)


def block_scale(own_key, extent, cuts, least, top_value):
    loudness = 1.0
    for position, shards_of in cuts:
        draws = jax.random.uniform(jax.random.fold_in(jax.random.fold_in(own_key, 6), position), (shards_of,), jnp.float32, least / len(cuts), top_value / len(cuts))
        loudness = loudness * jnp.repeat(jnp.exp(draws), extent[position] // shards_of).reshape((-1,) + (1,) * (len(extent) - 1 - position))
    return loudness


def gaussian(own_key, shape, deviation, reach, cuts=(), kind=jnp.bfloat16):
    result = jax.random.normal(own_key, shape, jnp.float32) * deviation
    if len(cuts) > 0:
        result = block_scale(own_key, shape, cuts, -0.22, 0.18) * result
    return jnp.clip(result, min=-reach, max=reach).astype(kind)


def setup_inputs(seed: int = 0) -> dict:
    key_of = jax.random.split(jax.random.key(seed), 8)
    arrived = gaussian(key_of[0], (3, TOKENS, D), 1.0, 6.0, ((1, 32),))
    landing = jax.vmap(lambda own: jax.random.permutation(own, N_SEQ))(jax.random.split(key_of[1], N_SEQ)).reshape((N_SEQ, N_SEQ)).astype(jnp.int32)
    resets = set_ends((jax.random.randint(key_of[2], (TOKENS,), 0, 8 * TOK_DEV) < 1).astype(jnp.int32), jax.random.fold_in(key_of[2], 1), 0, 1)
    short_taps = gaussian(key_of[3], (3, SHORT, D), 0.5, 3.0, ((2, 4),), jnp.float32)
    decay_rate = draw_decay_rate(jax.random.fold_in(key_of[7], 71), 0)
    residues = gaussian(key_of[5], (ORDER, D), 0.3, 2.0, ((1, 4),), jnp.float32)
    skip_gain = jnp.clip(0.5 + 1.0 * jax.random.uniform(key_of[6], (D,), jnp.float32) ** block_scale(key_of[6], (D,), ((0, 4),), -0.2, 0.2), 0.5, 1.5)
    return dict(arrived=arrived, landing=landing, resets=resets, short_taps=short_taps, decay_rate=decay_rate, residues=residues, skip_gain=skip_gain)


def causal_conv(values, tap_table):
    tap_count = tap_table.shape[0]
    length = values.shape[0]
    padded = jnp.concatenate([jnp.zeros((tap_count - 1, values.shape[1]), values.dtype), values], axis=0)

    def add_tap(tap_index, combined):
        shifted = lax.dynamic_slice_in_dim(padded, tap_count - 1 - tap_index, length, 0)
        return combined + tap_table[tap_index] * shifted
    return lax.fori_loop(0, tap_count, add_tap, jnp.zeros_like(values))

def reference(arrived, landing, resets, short_taps, decay_rate, residues, skip_gain):
    pieces = arrived.reshape(3, N_SEQ, N_SEQ, SLAB, D).transpose(0, 2, 1, 3, 4)
    sources = jnp.argsort(landing, axis=1).astype(jnp.int32)
    row_ids = jnp.arange(N_SEQ, dtype=jnp.int32)[:, None]
    ordered = pieces[:, row_ids, sources].reshape(3, TOKENS, D)
    front_conv = causal_conv(ordered[0].astype(jnp.float32), short_taps[0])
    key_conv = causal_conv(ordered[1].astype(jnp.float32), short_taps[1])
    value_conv = causal_conv(ordered[2].astype(jnp.float32), short_taps[2])
    gated_mix = (key_conv * value_conv).astype(jnp.bfloat16)
    gated_wide = gated_mix.astype(jnp.float32)
    decay_step = jnp.exp(-decay_rate)
    weight = residues * jnp.sqrt(-jnp.expm1(-2.0 * decay_rate))
    keep_mask = (1 - resets).astype(jnp.float32)

    def advance(carried_state, inputs):
        column, hold_flag = inputs
        carried_state = decay_step * carried_state * hold_flag + column[None, :]
        return (carried_state, lax.optimization_barrier(jnp.sum(weight * carried_state, axis=0)))
    _, modal_out = lax.scan(advance, jnp.zeros((ORDER, D), jnp.float32), (gated_wide, keep_mask))
    combined = modal_out + skip_gain[None, :] * gated_wide
    return (front_conv * combined).astype(jnp.bfloat16)
```

```python
import functools

import jax
import jax.numpy as jnp
from jax import lax
from jax.experimental import pallas as pl
from jax.experimental.pallas import tpu as pltpu
from jax.sharding import PartitionSpec as P

LANES = 128
SUBLANES = 8
GROUP = 8
CHUNKS = 4
VMEM_BYTES = 50 * 1024 * 1024

SMEM = pl.BlockSpec(memory_space=pltpu.SMEM)
VMEM = pl.BlockSpec(memory_space=pltpu.VMEM)
ANY = pl.BlockSpec(memory_space=pl.ANY)
PARAMS = pltpu.CompilerParams(vmem_limit_bytes=VMEM_BYTES)


def columns_of(table, chunk, width):
    lead = table.shape[:-1]
    return pl.BlockSpec((*lead, width), lambda g: (0,) * len(lead) + (chunk,))


def column_start(place_ref, d, chunk, width):
    return pl.multiple_of(((place_ref[0] ^ d) * CHUNKS + chunk) * width, LANES)


def cut_blocks(chunk, width, chans, place, arrived, later):

    def body(place_ref, arrived_ref, *refs):
        outs, sems = refs[len(later) : -1], refs[-1]
        copies = []
        for d, out in enumerate(outs, start=1):
            start = column_start(place_ref, d, chunk, width)
            copies.append(
                pltpu.make_async_copy(
                    arrived_ref.at[:, :, pl.ds(start, width)], out, sems.at[d - 1]
                )
            )
        for copy in copies:
            copy.start()
        for copy in copies:
            copy.wait()

    shape = jax.ShapeDtypeStruct((*arrived.shape[:2], width), arrived.dtype)
    return pl.pallas_call(
        body,
        in_specs=[SMEM, ANY] + [ANY] * len(later),
        out_specs=[VMEM] * (chans - 1),
        out_shape=[shape] * (chans - 1),
        scratch_shapes=[pltpu.SemaphoreType.DMA((chans - 1,))],
        compiler_params=PARAMS,
        name="cut_blocks",
    )(place, arrived, *later)


def shift_window(rows, start, count):
    return lax.slice_in_dim(rows, start, start + count, axis=0)


def cut_edges(place, arrived, per_device, reach, channels, chans):
    slab = arrived.shape[1] // per_device

    def body(place_ref, arrived_ref, *refs):
        outs, (tails, heads, sems) = refs[:chans], refs[chans:]
        copies = []
        for d in range(chans):
            start = pl.multiple_of((place_ref[0] ^ d) * channels, LANES)
            here = pl.ds(start, channels)
            for i in range(per_device):
                at = len(copies)
                copies.append(
                    pltpu.make_async_copy(
                        arrived_ref.at[:, pl.ds((i + 1) * slab - 16, 16), here],
                        tails.at[d, i],
                        sems.at[at],
                    )
                )
                copies.append(
                    pltpu.make_async_copy(
                        arrived_ref.at[2, pl.ds(i * slab, 16), here],
                        heads.at[d, i],
                        sems.at[at + 1],
                    )
                )
        for copy in copies:
            copy.start()
        for copy in copies:
            copy.wait()

        for d in range(chans):

            def one_block(block, carry, d=d):
                lanes = pl.ds(pl.multiple_of(block * LANES, LANES), LANES)
                for i in range(per_device):
                    parts = [
                        tails[d, i, k, :, lanes].astype(jnp.float32)[16 - reach :] for k in range(3)
                    ]
                    parts.append(heads[d, i, :, lanes].astype(jnp.float32)[:reach])
                    outs[d][i, :, lanes] = jnp.concatenate(parts, axis=0).astype(arrived.dtype)
                return carry

            lax.fori_loop(0, channels // LANES, one_block, 0)

    shape = jax.ShapeDtypeStruct((per_device, 4 * reach, channels), arrived.dtype)
    return pl.pallas_call(
        body,
        in_specs=[SMEM, ANY],
        out_specs=[VMEM] * chans,
        out_shape=[shape] * chans,
        scratch_shapes=[
            pltpu.VMEM((chans, per_device, 3, 16, channels), arrived.dtype),
            pltpu.VMEM((chans, per_device, 16, channels), arrived.dtype),
            pltpu.SemaphoreType.DMA((2 * chans * per_device,)),
        ],
        compiler_params=PARAMS,
        name="cut_edges",
    )(place, arrived)


def by_shard(place, parts, later):
    count = len(parts)
    per_device, rows, channels = parts[0].shape

    def body(place_ref, *refs):
        part_refs, (out_ref, sems) = refs[:count], refs[-2:]
        copies = [
            pltpu.make_async_copy(
                part_refs[d],
                out_ref.at[pl.ds((place_ref[0] ^ d) * per_device, per_device)],
                sems.at[d],
            )
            for d in range(count)
        ]
        for copy in copies:
            copy.start()
        for copy in copies:
            copy.wait()

    return pl.pallas_call(
        body,
        in_specs=[SMEM] + [ANY] * (count + len(later)),
        out_specs=VMEM,
        out_shape=jax.ShapeDtypeStruct((count * per_device, rows, channels), parts[0].dtype),
        scratch_shapes=[pltpu.SemaphoreType.DMA((count,))],
        compiler_params=PARAMS,
        name="by_shard",
    )(place, *parts, *later)


def front_body(chunk, count, place_ref, arrived_ref, *refs):
    block_refs = refs[: count - 1]
    taps_ref, out_ref, held, padded, sems = refs[-5:]
    shards, _, width = out_ref.shape
    per_device = shards // count
    slab = held.shape[2] // per_device
    taps = taps_ref.shape[1]
    reach = taps - 1
    blocks = width // LANES
    row_ids = lax.broadcasted_iota(jnp.int32, (slab, LANES), 0)
    sources = [arrived_ref.at[:, :, pl.ds(column_start(place_ref, 0, chunk, width), width)]]
    sources += block_refs
    copies = [pltpu.make_async_copy(sources[d], held.at[d], sems.at[d]) for d in range(count)]
    for copy in copies:
        copy.start()
    for k in range(3):
        padded[k, :8, :] = jnp.zeros((8, LANES), jnp.float32)
    for d in range(count):
        copies[d].wait()

        def one_block(step, carry, d=d):
            i, block = step // blocks, step % blocks
            lanes = pl.ds(pl.multiple_of(block * LANES, LANES), LANES)
            own = pl.ds(pl.multiple_of(i * slab, slab), slab)
            shard = (place_ref[0] ^ d) * per_device + i

            def conv(k):
                rows = held[d, k, own, lanes].astype(jnp.float32)
                padded[k, 8:, :] = rows
                total = taps_ref[k, 0:1, lanes] * rows
                for j in range(1, taps):
                    total = total + taps_ref[k, j : j + 1, lanes] * padded[k, 8 - j : 8 - j + slab, :]
                return total

            front = conv(0)
            key = conv(1)
            value = conv(2)
            gate = jnp.where(row_ids < reach, key, key * value)
            out_ref[shard, :slab, lanes] = front.astype(out_ref.dtype)
            out_ref[shard, slab:, lanes] = gate.astype(out_ref.dtype)
            return carry

        lax.fori_loop(0, per_device * blocks, one_block, 0)


def slab_fronts(chunk, width, place, arrived, blocks, taps, per_device, after):
    count = len(blocks) + 1
    rows = arrived.shape[1]
    shape = (count * per_device, 2 * (rows // per_device), width)
    return pl.pallas_call(
        functools.partial(front_body, chunk, count),
        grid=(1,),
        in_specs=[SMEM] + [ANY] * (count + len(after)) + [columns_of(taps, chunk, width)],
        out_specs=pl.BlockSpec(shape, lambda g: (0, 0, 0)),
        out_shape=jax.ShapeDtypeStruct(shape, arrived.dtype),
        scratch_shapes=[
            pltpu.VMEM((count, 3, rows, width), arrived.dtype),
            pltpu.VMEM((3, rows // per_device + 8, LANES), jnp.float32),
            pltpu.SemaphoreType.DMA((count,)),
        ],
        compiler_params=PARAMS,
        cost_estimate=pl.CostEstimate(
            flops=60 * count * rows * width,
            bytes_accessed=10 * count * rows * width,
            transcendentals=0,
        ),
        name="slab_fronts",
    )(place, arrived, *blocks, *after, taps)


def spread(values, blocks):
    if len(values) == 1:
        return values[0]
    ids = lax.broadcasted_iota(jnp.int32, (len(values) * blocks, LANES), 0)
    out = jnp.full(ids.shape, values[-1])
    for g in range(len(values) - 2, -1, -1):
        out = jnp.where(ids < (g + 1) * blocks, values[g], out)
    return out


def mode_rows(ref, table, n, sub):
    return ref[table, n * sub : (n + 1) * sub, :]


def scan_body(chunk, segments, shared, *refs):
    slots_ref, resets_ref, busy_ref, clear_ref, slab_ref, edge_ref, before_ref = refs[:7]
    taps_ref, decay_ref, gain_ref, skip_ref, across_ref = refs[7:12]
    earlier_refs = refs[12 : 12 + (shared > 0)]
    front_ref, local_ref, base_ref, ended_ref = refs[12 + shared : 16 + shared]
    slabs, edges, wide, by_mode, sems = refs[16 + shared :]
    count, rows, width = slabs.shape
    taps = taps_ref.shape[1]
    reach = taps - 1
    slab = rows // 2
    modes = decay_ref.shape[0]
    blocks = width // LANES
    sub = segments * blocks
    steps = count * slab // segments

    here = pl.ds(chunk * width, width)
    copies = [pltpu.make_async_copy(before_ref.at[:, here], edges.at[0], sems.at[2 * count])]
    for m in range(count):
        slot = slots_ref[m]
        copies.append(pltpu.make_async_copy(slab_ref.at[m], slabs.at[slot], sems.at[m]))
        copies.append(
            pltpu.make_async_copy(
                edge_ref.at[m, :, here], edges.at[slot + 1], sems.at[count + m]
            )
        )
    for copy in copies:
        copy.start()
    for g in range(segments):
        for j in range(blocks):
            lanes = slice(j * LANES, (j + 1) * LANES)
            at = g * blocks + j
            by_mode[0, pl.ds(at, modes, stride=sub), :] = decay_ref[:, lanes]
            by_mode[1, pl.ds(at, modes, stride=sub), :] = gain_ref[:, lanes]
            by_mode[2, at : at + 1, :] = skip_ref[:, lanes]
    for ref in earlier_refs:
        ended_ref[:, : chunk * width] = ref[:, : chunk * width]
    for copy in copies:
        copy.wait()

    row_ids = lax.broadcasted_iota(jnp.int32, (slab, LANES), 0)
    blank = jnp.zeros((16 - reach, LANES), jnp.float32)

    def one_slot(slot, carry):
        first = slot * slab
        g, t = first // steps, first % steps
        for j in range(blocks):
            lanes = slice(j * LANES, (j + 1) * LANES)
            edge = edges[slot, :, lanes].astype(jnp.float32)
            own = edges[slot + 1, :, lanes].astype(jnp.float32)

            def from_rows(k, rows, least):
                total = jnp.zeros((8, LANES), jnp.float32)
                for tap in range(least, taps):
                    total = total + taps_ref[k, tap : tap + 1, lanes] * shift_window(
                        rows, reach - tap, 8
                    )
                return total

            def tail(k):
                return edge[k * reach : (k + 1) * reach]

            add_front = from_rows(0, jnp.concatenate([tail(0), blank], axis=0), 1)
            add_key = from_rows(1, jnp.concatenate([tail(1), blank], axis=0), 1)
            value = from_rows(
                2, jnp.concatenate([tail(2), own[3 * reach :], blank[reach:]], axis=0), 0
            )
            starts = row_ids[:8] < reach
            front = slabs[slot, :slab, lanes].astype(jnp.float32)
            gate = slabs[slot, slab:, lanes].astype(jnp.float32)
            front_start = jnp.where(starts, front[:8] + add_front, front[:8])
            gate_start = ((gate[:8] + add_key) * value).astype(jnp.bfloat16)
            gate_start = jnp.where(starts, gate_start.astype(jnp.float32), gate[:8])
            front = jnp.concatenate([front_start, front[8:]], axis=0)
            gate = jnp.concatenate([gate_start, gate[8:]], axis=0)
            base = pl.multiple_of(first, slab)
            front_ref[pl.ds(base, slab), lanes] = front.astype(front_ref.dtype)
            wide[pl.ds(t * sub + (g * blocks + j), slab, stride=sub), :] = gate

        return carry

    lax.fori_loop(0, count, one_slot, 0)

    decay = [mode_rows(by_mode, 0, n, sub) for n in range(modes)]
    gain = [mode_rows(by_mode, 1, n, sub) for n in range(modes)]
    skip = by_mode[2, 0:sub, :]

    def tokens(step, states, with_resets):
        states = list(states)
        for u in range(GROUP):
            token = step * GROUP + u
            at = pl.ds(pl.multiple_of(token * sub, sub), sub)
            if with_resets:
                hold = spread(
                    [
                        jnp.where(resets_ref[g * steps + token] == 0, 1.0, 0.0)
                        for g in range(segments)
                    ],
                    blocks,
                )
                states = [state * hold for state in states]
            gate = wide[at, :]
            sums = [skip * gate, None]
            for n in range(modes):
                states[n] = states[n] * decay[n] + gate
                term = gain[n] * states[n]
                sums[n % 2] = term if sums[n % 2] is None else sums[n % 2] + term
            local_ref[at, :] = sums[0] + sums[1]
        return tuple(states)

    def some_tokens(step, states):
        return lax.cond(
            busy_ref[step] == 0,
            lambda held: tokens(step, held, False),
            lambda held: tokens(step, held, True),
            states,
        )

    zero = jnp.zeros((sub, LANES), jnp.float32)
    states = lax.fori_loop(0, steps // GROUP, some_tokens, (zero,) * modes)
    for n in range(modes):
        by_mode[0, n * sub : (n + 1) * sub, :] = states[n]
    open_shard = clear_ref[0]
    for g in range(1, segments):
        open_shard = open_shard * clear_ref[g]
    for j in range(blocks):
        lanes = slice(j * LANES, (j + 1) * LANES)
        entering = jnp.zeros((modes, LANES), jnp.float32)
        for g in range(segments):
            base_ref[g, :, lanes] = entering
            ended = by_mode[0, pl.ds(g * blocks + j, modes, stride=sub), :]
            entering = ended + across_ref[:, lanes] * clear_ref[g] * entering
        ended_ref[:, chunk * width + j * LANES : chunk * width + (j + 1) * LANES] = (
            entering.astype(ended_ref.dtype)
        )
    ended_ref[:, (chunk + 1) * width :] = jnp.full(
        (modes, LANES), open_shard, jnp.float32
    ).astype(ended_ref.dtype)


def whole_block(shape):
    return pl.BlockSpec(shape, lambda g: (0,) * len(shape))


def scan_shard(
    chunk, width, segments, slots, resets, busy, clear, slabs, edges, before, tables, earlier
):
    count, rows, _ = slabs.shape
    length = resets.shape[0]
    modes, channels = tables[1].shape
    blocks = width // LANES
    sub = segments * blocks
    outs = [
        jax.ShapeDtypeStruct((length, channels), jnp.bfloat16),
        jax.ShapeDtypeStruct((length * channels // LANES, LANES), jnp.float32),
        jax.ShapeDtypeStruct((segments, modes, channels), jnp.float32),
        jax.ShapeDtypeStruct((modes, (chunk + 1) * width + LANES), jnp.bfloat16),
    ]
    shared = [*earlier[3:], *earlier[:3]]
    first = 7 + len(tables) + 1
    return pl.pallas_call(
        functools.partial(scan_body, chunk, segments, len(shared)),
        grid=(1,),
        in_specs=[SMEM] * 4 + [ANY] * 3
        + [columns_of(table, chunk, width) for table in tables]
        + [whole_block(value.shape) for value in shared[:1]]
        + [ANY] * len(shared[1:]),
        out_specs=[
            columns_of(outs[0], chunk, width),
            pl.BlockSpec((length * blocks, LANES), lambda g: (chunk, 0)),
            columns_of(outs[2], chunk, width),
            whole_block(outs[3].shape),
        ],
        out_shape=outs,
        input_output_aliases={first + i: i for i in range(len(shared[1:]))},
        scratch_shapes=[
            pltpu.VMEM((count, rows, width), jnp.bfloat16),
            pltpu.VMEM((count + 1, edges.shape[1], width), jnp.bfloat16),
            pltpu.VMEM((length * blocks, LANES), jnp.float32),
            pltpu.VMEM((3, modes * sub, LANES), jnp.float32),
            pltpu.SemaphoreType.DMA((2 * count + 1,)),
        ],
        compiler_params=PARAMS,
        cost_estimate=pl.CostEstimate(
            flops=100 * length * width, bytes_accessed=10 * length * width, transcendentals=0
        ),
        name="scan_shard",
    )(slots, resets, busy, clear, slabs, edges, before, *tables, *shared)


def carry_body(segments, count, *refs):
    limit_ref, clear_ref = refs[:2]
    end_refs = refs[2 : 2 + count]
    through_ref, across_ref, decay_ref, gain_ref = refs[2 + count : 6 + count]
    base_ref, front_ref, local_ref = refs[6 + count : 9 + count]
    out_ref, by_mode, carried = refs[-3:]
    modes, width = decay_ref.shape
    length = front_ref.shape[0]
    blocks = width // LANES
    sub = segments * blocks
    steps = length // segments
    part = min(64, steps)
    for j in range(blocks):
        lanes = slice(j * LANES, (j + 1) * LANES)
        here = pl.ds(pl.multiple_of(pl.program_id(0) * width + j * LANES, LANES), LANES)
        entering = jnp.zeros((modes, LANES), jnp.float32)
        for ref in reversed(end_refs):
            is_open = ref[:, ref.shape[1] - LANES :].astype(jnp.float32)
            entering = ref[:, here].astype(jnp.float32) + (
                through_ref[:, lanes] * is_open * entering
            )
        for g in range(segments):
            at = pl.ds(g * blocks + j, modes, stride=sub)
            by_mode[0, at, :] = decay_ref[:, lanes]
            by_mode[1, at, :] = gain_ref[:, lanes] * (base_ref[g, :, lanes] + entering)
            entering = entering * across_ref[:, lanes] * clear_ref[g]
    decay = [mode_rows(by_mode, 0, n, sub) for n in range(modes)]
    limit = spread([jnp.full((sub, LANES), limit_ref[g]) for g in range(segments)], blocks)

    def some_tokens(step, states):
        states = list(states)
        for u in range(GROUP):
            token = step * GROUP + u
            at = pl.ds(pl.multiple_of(token * sub, sub), sub)
            sums = [None] * 4
            for n in range(modes):
                states[n] = states[n] * decay[n]
                sums[n % 4] = states[n] if sums[n % 4] is None else sums[n % 4] + states[n]
            added = (sums[0] + sums[1]) + (sums[2] + sums[3])
            carried[at, :] = local_ref[at, :] + jnp.where(token < limit, added, 0.0)
        return tuple(states)

    lax.fori_loop(
        0,
        steps // GROUP,
        some_tokens,
        tuple(mode_rows(by_mode, 1, n, sub) for n in range(modes)),
    )

    def finish(step, carry):
        first = step * part
        g, t = first // steps, first % steps
        rows = pl.ds(pl.multiple_of(first, part), part)
        for j in range(blocks):
            lanes = slice(j * LANES, (j + 1) * LANES)
            total = carried[pl.ds(t * sub + (g * blocks + j), part, stride=sub), :]
            out_ref[rows, lanes] = (front_ref[rows, lanes].astype(jnp.float32) * total).astype(
                out_ref.dtype
            )
        return carry

    lax.fori_loop(0, length // part, finish, 0)


def carry_shard(width, segments, limit, clear, ends, tables, base, front, local):
    length, channels = front.shape
    modes = tables[0].shape[0]
    blocks = width // LANES
    sub = segments * blocks
    specs = [SMEM, SMEM]
    specs += [whole_block(value.shape) for value in ends]
    specs += [pl.BlockSpec((modes, width), lambda g: (0, g)) for table in tables]
    specs.append(pl.BlockSpec((segments, modes, width), lambda g: (0, 0, g)))
    specs.append(pl.BlockSpec((length, width), lambda g: (0, g)))
    specs.append(pl.BlockSpec((length * blocks, LANES), lambda g: (g, 0)))
    return pl.pallas_call(
        functools.partial(carry_body, segments, len(ends)),
        grid=(channels // width,),
        in_specs=specs,
        out_specs=pl.BlockSpec((length, width), lambda g: (0, g)),
        out_shape=jax.ShapeDtypeStruct((length, channels), jnp.bfloat16),
        scratch_shapes=[
            pltpu.VMEM((2, modes * sub, LANES), jnp.float32),
            pltpu.VMEM((length * blocks, LANES), jnp.float32),
        ],
        compiler_params=PARAMS,
        cost_estimate=pl.CostEstimate(
            flops=40 * length * channels, bytes_accessed=8 * length * channels, transcendentals=0
        ),
        name="carry_shard",
    )(limit, clear, *ends, *tables, base, front, local)


def on_device(arrived, landing, resets, short_taps, decay_rate, residues, skip_gain):
    shards, chans = lax.axis_size("seq"), lax.axis_size("chan")
    chan = lax.axis_index("chan")
    per_device = shards // chans
    length = resets.shape[0]
    channels = short_taps.shape[2]
    reach = short_taps.shape[1] - 1
    width = channels // CHUNKS
    segments = max(1, SUBLANES * LANES // width)

    def passed_along(value, by):
        return lax.ppermute(value, "seq", [(i, i + by) for i in range(shards - by)])

    place = chan.astype(jnp.int32)[None]
    slots = landing[0]
    final = jnp.argmax(slots == shards - 1)
    marks = resets.reshape(segments, -1)
    steps = marks.shape[1]
    limit = jnp.min(
        jnp.where(marks != 0, lax.broadcasted_iota(jnp.int32, marks.shape, 1), steps), axis=1
    )
    clear = (limit == steps).astype(jnp.float32)
    busy = jnp.sum(marks.reshape(segments, -1, GROUP), axis=(0, 2))
    decay = jnp.exp(-decay_rate)
    through = jnp.exp(-decay_rate * length)
    across = jnp.exp(-decay_rate * steps)
    gain = residues * jnp.sqrt(-jnp.expm1(-2.0 * decay_rate))
    skip = skip_gain[None]

    def across_plane(parts):
        return [
            lax.ppermute(part, "chan", [(c, c ^ d) for c in range(chans)])
            for d, part in enumerate(parts, start=1)
        ]

    def along_column(value):
        return lax.all_to_all(value, "seq", split_axis=0, concat_axis=0, tiled=True)

    own, *parts = cut_edges(place, arrived, per_device, reach, channels, chans)
    parts = [own, *across_plane(parts)]
    cuts = [cut_blocks(0, width, chans, place, arrived, [own])]
    edges = along_column(by_shard(place, parts, cuts[0]))
    last = lax.dynamic_index_in_dim(edges, final, axis=0, keepdims=False)
    before = passed_along(last, 1)

    scanned, ended = [], []
    for chunk in range(CHUNKS):
        blocks = across_plane(cuts[chunk])
        ready = [before] if chunk == 0 else ended[chunk - 2 : chunk - 1]
        if 0 < chunk < CHUNKS - 1:
            cuts.append(cut_blocks(chunk + 1, width, chans, place, arrived, [sent]))
            ready = [*ready, cuts[-1][0]]
        sent = slab_fronts(
            chunk, width, place, arrived, blocks, short_taps, per_device, ready
        )
        if chunk == 0:
            cuts.append(cut_blocks(1, width, chans, place, arrived, [sent]))
        scanned = scan_shard(
            chunk,
            width,
            segments,
            slots,
            resets,
            busy,
            clear,
            along_column(sent),
            edges,
            before,
            (short_taps, decay, gain, skip, across),
            scanned,
        )
        ended.append(scanned[3])
    front, local, base, _ = scanned
    ends = [passed_along(ended[-1], d) for d in range(1, shards)]
    return carry_shard(
        width, segments, limit, clear, ends, (through, across, decay, gain), base, front, local
    )


def solution(mesh):
    in_specs = (
        P(None, ("seq", "chan"), None),
        P("seq", None),
        P("seq"),
        P(None, None, "chan"),
        P(None, "chan"),
        P(None, "chan"),
        P("chan"),
    )
    out_specs = P("seq", "chan")
    return jax.shard_map(
        on_device, mesh=mesh, in_specs=in_specs, out_specs=out_specs, check_vma=False
    )
```

```python
import functools

import jax
import jax.numpy as jnp
from jax import lax
from jax.experimental import pallas as pl
from jax.experimental.pallas import tpu as pltpu
from jax.sharding import PartitionSpec as P

LANES = 128
SUBLANES = 8
GROUP = 16
CHUNKS = 4
VMEM_BYTES = 50 * 1024 * 1024

SMEM = pl.BlockSpec(memory_space=pltpu.SMEM)
VMEM = pl.BlockSpec(memory_space=pltpu.VMEM)
ANY = pl.BlockSpec(memory_space=pl.ANY)
PARAMS = pltpu.CompilerParams(vmem_limit_bytes=VMEM_BYTES)


def columns_of(table, chunk, width):
    lead = table.shape[:-1]
    return pl.BlockSpec((*lead, width), lambda g: (0,) * len(lead) + (chunk,))


def column_start(place_ref, d, chunk, width):
    return pl.multiple_of(((place_ref[0] ^ d) * CHUNKS + chunk) * width, LANES)


def cut_blocks(chunk, width, chans, place, arrived, later):

    def body(place_ref, arrived_ref, *refs):
        outs, sems = refs[len(later) : -1], refs[-1]
        copies = []
        for d, out in enumerate(outs, start=1):
            start = column_start(place_ref, d, chunk, width)
            copies.append(
                pltpu.make_async_copy(
                    arrived_ref.at[:, :, pl.ds(start, width)], out, sems.at[d - 1]
                )
            )
        for copy in copies:
            copy.start()
        for copy in copies:
            copy.wait()

    shape = jax.ShapeDtypeStruct((*arrived.shape[:2], width), arrived.dtype)
    return pl.pallas_call(
        body,
        in_specs=[SMEM, ANY] + [ANY] * len(later),
        out_specs=[VMEM] * (chans - 1),
        out_shape=[shape] * (chans - 1),
        scratch_shapes=[pltpu.SemaphoreType.DMA((chans - 1,))],
        compiler_params=PARAMS,
        name="cut_blocks",
    )(place, arrived, *later)


def shift_window(rows, start, count):
    return lax.slice_in_dim(rows, start, start + count, axis=0)


def cut_edges(place, arrived, per_device, reach, channels, chans):
    slab = arrived.shape[1] // per_device

    def body(place_ref, arrived_ref, *refs):
        outs, (tails, heads, sems) = refs[:chans], refs[chans:]
        copies = []
        for d in range(chans):
            start = pl.multiple_of((place_ref[0] ^ d) * channels, LANES)
            here = pl.ds(start, channels)
            for i in range(per_device):
                at = len(copies)
                copies.append(
                    pltpu.make_async_copy(
                        arrived_ref.at[:, pl.ds((i + 1) * slab - 16, 16), here],
                        tails.at[d, i],
                        sems.at[at],
                    )
                )
                copies.append(
                    pltpu.make_async_copy(
                        arrived_ref.at[2, pl.ds(i * slab, 16), here],
                        heads.at[d, i],
                        sems.at[at + 1],
                    )
                )
        for copy in copies:
            copy.start()
        for copy in copies:
            copy.wait()

        for d in range(chans):

            def one_block(block, carry, d=d):
                lanes = pl.ds(pl.multiple_of(block * LANES, LANES), LANES)
                for i in range(per_device):
                    parts = [
                        tails[d, i, k, :, lanes].astype(jnp.float32)[16 - reach :] for k in range(3)
                    ]
                    parts.append(heads[d, i, :, lanes].astype(jnp.float32)[:reach])
                    outs[d][i, :, lanes] = jnp.concatenate(parts, axis=0).astype(arrived.dtype)
                return carry

            lax.fori_loop(0, channels // LANES, one_block, 0)

    shape = jax.ShapeDtypeStruct((per_device, 4 * reach, channels), arrived.dtype)
    return pl.pallas_call(
        body,
        in_specs=[SMEM, ANY],
        out_specs=[VMEM] * chans,
        out_shape=[shape] * chans,
        scratch_shapes=[
            pltpu.VMEM((chans, per_device, 3, 16, channels), arrived.dtype),
            pltpu.VMEM((chans, per_device, 16, channels), arrived.dtype),
            pltpu.SemaphoreType.DMA((2 * chans * per_device,)),
        ],
        compiler_params=PARAMS,
        name="cut_edges",
    )(place, arrived)


def by_shard(place, parts, later):
    count = len(parts)
    per_device, rows, channels = parts[0].shape

    def body(place_ref, *refs):
        part_refs, (out_ref, sems) = refs[:count], refs[-2:]
        copies = [
            pltpu.make_async_copy(
                part_refs[d],
                out_ref.at[pl.ds((place_ref[0] ^ d) * per_device, per_device)],
                sems.at[d],
            )
            for d in range(count)
        ]
        for copy in copies:
            copy.start()
        for copy in copies:
            copy.wait()

    return pl.pallas_call(
        body,
        in_specs=[SMEM] + [ANY] * (count + len(later)),
        out_specs=VMEM,
        out_shape=jax.ShapeDtypeStruct((count * per_device, rows, channels), parts[0].dtype),
        scratch_shapes=[pltpu.SemaphoreType.DMA((count,))],
        compiler_params=PARAMS,
        name="by_shard",
    )(place, *parts, *later)


def front_body(chunk, count, place_ref, arrived_ref, *refs):
    block_refs = refs[: count - 1]
    taps_ref, out_ref, held, padded, sems = refs[-5:]
    shards, _, width = out_ref.shape
    per_device = shards // count
    slab = held.shape[2] // per_device
    taps = taps_ref.shape[1]
    reach = taps - 1
    blocks = width // LANES
    row_ids = lax.broadcasted_iota(jnp.int32, (slab, LANES), 0)
    sources = [arrived_ref.at[:, :, pl.ds(column_start(place_ref, 0, chunk, width), width)]]
    sources += block_refs
    copies = [pltpu.make_async_copy(sources[d], held.at[d], sems.at[d]) for d in range(count)]
    for copy in copies:
        copy.start()
    for k in range(3):
        padded[k, :8, :] = jnp.zeros((8, LANES), jnp.float32)
    for d in range(count):
        copies[d].wait()

        def one_block(step, carry, d=d):
            i, block = step // blocks, step % blocks
            lanes = pl.ds(pl.multiple_of(block * LANES, LANES), LANES)
            own = pl.ds(pl.multiple_of(i * slab, slab), slab)
            shard = (place_ref[0] ^ d) * per_device + i

            def conv(k):
                rows = held[d, k, own, lanes].astype(jnp.float32)
                padded[k, 8:, :] = rows
                total = taps_ref[k, 0:1, lanes] * rows
                for j in range(1, taps):
                    total = total + taps_ref[k, j : j + 1, lanes] * padded[k, 8 - j : 8 - j + slab, :]
                return total

            front = conv(0)
            key = conv(1)
            value = conv(2)
            gate = jnp.where(row_ids < reach, key, key * value)
            out_ref[shard, :slab, lanes] = front.astype(out_ref.dtype)
            out_ref[shard, slab:, lanes] = gate.astype(out_ref.dtype)
            return carry

        lax.fori_loop(0, per_device * blocks, one_block, 0)


def slab_fronts(chunk, width, place, arrived, blocks, taps, per_device, after):
    count = len(blocks) + 1
    rows = arrived.shape[1]
    shape = (count * per_device, 2 * (rows // per_device), width)
    return pl.pallas_call(
        functools.partial(front_body, chunk, count),
        grid=(1,),
        in_specs=[SMEM] + [ANY] * (count + len(after)) + [columns_of(taps, chunk, width)],
        out_specs=pl.BlockSpec(shape, lambda g: (0, 0, 0)),
        out_shape=jax.ShapeDtypeStruct(shape, arrived.dtype),
        scratch_shapes=[
            pltpu.VMEM((count, 3, rows, width), arrived.dtype),
            pltpu.VMEM((3, rows // per_device + 8, LANES), jnp.float32),
            pltpu.SemaphoreType.DMA((count,)),
        ],
        compiler_params=PARAMS,
        cost_estimate=pl.CostEstimate(
            flops=60 * count * rows * width,
            bytes_accessed=10 * count * rows * width,
            transcendentals=0,
        ),
        name="slab_fronts",
    )(place, arrived, *blocks, *after, taps)


def spread(values, blocks):
    if len(values) == 1:
        return values[0]
    ids = lax.broadcasted_iota(jnp.int32, (len(values) * blocks, LANES), 0)
    out = jnp.full(ids.shape, values[-1])
    for g in range(len(values) - 2, -1, -1):
        out = jnp.where(ids < (g + 1) * blocks, values[g], out)
    return out


def mode_rows(ref, table, n, sub):
    return ref[table, n * sub : (n + 1) * sub, :]


def scan_body(chunk, segments, shared, *refs):
    slots_ref, resets_ref, busy_ref, clear_ref, slab_ref, edge_ref, before_ref = refs[:7]
    taps_ref, decay_ref, gain_ref, skip_ref, across_ref = refs[7:12]
    earlier_refs = refs[12 : 12 + (shared > 0)]
    front_ref, local_ref, base_ref, ended_ref = refs[12 + shared : 16 + shared]
    slabs, edges, wide, by_mode, sems = refs[16 + shared :]
    count, rows, width = slabs.shape
    taps = taps_ref.shape[1]
    reach = taps - 1
    slab = rows // 2
    modes = decay_ref.shape[0]
    blocks = width // LANES
    sub = segments * blocks
    steps = count * slab // segments

    here = pl.ds(chunk * width, width)
    copies = [pltpu.make_async_copy(before_ref.at[:, here], edges.at[0], sems.at[2 * count])]
    for m in range(count):
        slot = slots_ref[m]
        copies.append(pltpu.make_async_copy(slab_ref.at[m], slabs.at[slot], sems.at[m]))
        copies.append(
            pltpu.make_async_copy(
                edge_ref.at[m, :, here], edges.at[slot + 1], sems.at[count + m]
            )
        )
    for copy in copies:
        copy.start()
    for g in range(segments):
        for j in range(blocks):
            lanes = slice(j * LANES, (j + 1) * LANES)
            at = g * blocks + j
            by_mode[0, pl.ds(at, modes, stride=sub), :] = decay_ref[:, lanes]
            by_mode[1, pl.ds(at, modes, stride=sub), :] = gain_ref[:, lanes]
            by_mode[2, at : at + 1, :] = skip_ref[:, lanes]
    for ref in earlier_refs:
        ended_ref[:, : chunk * width] = ref[:, : chunk * width]
    for copy in copies:
        copy.wait()

    row_ids = lax.broadcasted_iota(jnp.int32, (slab, LANES), 0)
    blank = jnp.zeros((16 - reach, LANES), jnp.float32)

    def one_slot(slot, carry):
        first = slot * slab
        g, t = first // steps, first % steps
        for j in range(blocks):
            lanes = slice(j * LANES, (j + 1) * LANES)
            edge = edges[slot, :, lanes].astype(jnp.float32)
            own = edges[slot + 1, :, lanes].astype(jnp.float32)

            def from_rows(k, rows, least):
                total = jnp.zeros((8, LANES), jnp.float32)
                for tap in range(least, taps):
                    total = total + taps_ref[k, tap : tap + 1, lanes] * shift_window(
                        rows, reach - tap, 8
                    )
                return total

            def tail(k):
                return edge[k * reach : (k + 1) * reach]

            add_front = from_rows(0, jnp.concatenate([tail(0), blank], axis=0), 1)
            add_key = from_rows(1, jnp.concatenate([tail(1), blank], axis=0), 1)
            value = from_rows(
                2, jnp.concatenate([tail(2), own[3 * reach :], blank[reach:]], axis=0), 0
            )
            starts = row_ids[:8] < reach
            front = slabs[slot, :slab, lanes].astype(jnp.float32)
            gate = slabs[slot, slab:, lanes].astype(jnp.float32)
            front_start = jnp.where(starts, front[:8] + add_front, front[:8])
            gate_start = ((gate[:8] + add_key) * value).astype(jnp.bfloat16)
            gate_start = jnp.where(starts, gate_start.astype(jnp.float32), gate[:8])
            front = jnp.concatenate([front_start, front[8:]], axis=0)
            gate = jnp.concatenate([gate_start, gate[8:]], axis=0)
            base = pl.multiple_of(first, slab)
            front_ref[pl.ds(base, slab), lanes] = front.astype(front_ref.dtype)
            wide[pl.ds(t * sub + (g * blocks + j), slab, stride=sub), :] = gate

        return carry

    lax.fori_loop(0, count, one_slot, 0)

    decay = [mode_rows(by_mode, 0, n, sub) for n in range(modes)]
    gain = [mode_rows(by_mode, 1, n, sub) for n in range(modes)]
    skip = by_mode[2, 0:sub, :]

    def tokens(step, states, with_resets):
        states = list(states)
        for u in range(GROUP):
            token = step * GROUP + u
            at = pl.ds(pl.multiple_of(token * sub, sub), sub)
            if with_resets:
                hold = spread(
                    [
                        jnp.where(resets_ref[g * steps + token] == 0, 1.0, 0.0)
                        for g in range(segments)
                    ],
                    blocks,
                )
                states = [state * hold for state in states]
            gate = wide[at, :]
            sums = [skip * gate, None]
            for n in range(modes):
                states[n] = states[n] * decay[n] + gate
                term = gain[n] * states[n]
                sums[n % 2] = term if sums[n % 2] is None else sums[n % 2] + term
            local_ref[at, :] = sums[0] + sums[1]
        return tuple(states)

    def some_tokens(step, states):
        return lax.cond(
            busy_ref[step] == 0,
            lambda held: tokens(step, held, False),
            lambda held: tokens(step, held, True),
            states,
        )

    zero = jnp.zeros((sub, LANES), jnp.float32)
    states = lax.fori_loop(0, steps // GROUP, some_tokens, (zero,) * modes)
    for n in range(modes):
        by_mode[0, n * sub : (n + 1) * sub, :] = states[n]
    open_shard = clear_ref[0]
    for g in range(1, segments):
        open_shard = open_shard * clear_ref[g]
    for j in range(blocks):
        lanes = slice(j * LANES, (j + 1) * LANES)
        entering = jnp.zeros((modes, LANES), jnp.float32)
        for g in range(segments):
            base_ref[g, :, lanes] = entering
            ended = by_mode[0, pl.ds(g * blocks + j, modes, stride=sub), :]
            entering = ended + across_ref[:, lanes] * clear_ref[g] * entering
        ended_ref[:, chunk * width + j * LANES : chunk * width + (j + 1) * LANES] = (
            entering.astype(ended_ref.dtype)
        )
    ended_ref[:, (chunk + 1) * width :] = jnp.full(
        (modes, LANES), open_shard, jnp.float32
    ).astype(ended_ref.dtype)


def whole_block(shape):
    return pl.BlockSpec(shape, lambda g: (0,) * len(shape))


def scan_shard(
    chunk, width, segments, slots, resets, busy, clear, slabs, edges, before, tables, earlier
):
    count, rows, _ = slabs.shape
    length = resets.shape[0]
    modes, channels = tables[1].shape
    blocks = width // LANES
    sub = segments * blocks
    outs = [
        jax.ShapeDtypeStruct((length, channels), jnp.bfloat16),
        jax.ShapeDtypeStruct((length * channels // LANES, LANES), jnp.float32),
        jax.ShapeDtypeStruct((segments, modes, channels), jnp.float32),
        jax.ShapeDtypeStruct((modes, (chunk + 1) * width + LANES), jnp.bfloat16),
    ]
    shared = [*earlier[3:], *earlier[:3]]
    first = 7 + len(tables) + 1
    return pl.pallas_call(
        functools.partial(scan_body, chunk, segments, len(shared)),
        grid=(1,),
        in_specs=[SMEM] * 4 + [ANY] * 3
        + [columns_of(table, chunk, width) for table in tables]
        + [whole_block(value.shape) for value in shared[:1]]
        + [ANY] * len(shared[1:]),
        out_specs=[
            columns_of(outs[0], chunk, width),
            pl.BlockSpec((length * blocks, LANES), lambda g: (chunk, 0)),
            columns_of(outs[2], chunk, width),
            whole_block(outs[3].shape),
        ],
        out_shape=outs,
        input_output_aliases={first + i: i for i in range(len(shared[1:]))},
        scratch_shapes=[
            pltpu.VMEM((count, rows, width), jnp.bfloat16),
            pltpu.VMEM((count + 1, edges.shape[1], width), jnp.bfloat16),
            pltpu.VMEM((length * blocks, LANES), jnp.float32),
            pltpu.VMEM((3, modes * sub, LANES), jnp.float32),
            pltpu.SemaphoreType.DMA((2 * count + 1,)),
        ],
        compiler_params=PARAMS,
        cost_estimate=pl.CostEstimate(
            flops=100 * length * width, bytes_accessed=10 * length * width, transcendentals=0
        ),
        name="scan_shard",
    )(slots, resets, busy, clear, slabs, edges, before, *tables, *shared)


def carry_body(segments, count, *refs):
    limit_ref, clear_ref = refs[:2]
    end_refs = refs[2 : 2 + count]
    through_ref, across_ref, decay_ref, gain_ref = refs[2 + count : 6 + count]
    base_ref, front_ref, local_ref = refs[6 + count : 9 + count]
    out_ref, by_mode, carried = refs[-3:]
    modes, width = decay_ref.shape
    length = front_ref.shape[0]
    blocks = width // LANES
    sub = segments * blocks
    steps = length // segments
    part = min(64, steps)
    for j in range(blocks):
        lanes = slice(j * LANES, (j + 1) * LANES)
        here = pl.ds(pl.multiple_of(pl.program_id(0) * width + j * LANES, LANES), LANES)
        entering = jnp.zeros((modes, LANES), jnp.float32)
        for ref in reversed(end_refs):
            is_open = ref[:, ref.shape[1] - LANES :].astype(jnp.float32)
            entering = ref[:, here].astype(jnp.float32) + (
                through_ref[:, lanes] * is_open * entering
            )
        for g in range(segments):
            at = pl.ds(g * blocks + j, modes, stride=sub)
            by_mode[0, at, :] = decay_ref[:, lanes]
            by_mode[1, at, :] = gain_ref[:, lanes] * (base_ref[g, :, lanes] + entering)
            entering = entering * across_ref[:, lanes] * clear_ref[g]
    decay = [mode_rows(by_mode, 0, n, sub) for n in range(modes)]
    limit = spread([jnp.full((sub, LANES), limit_ref[g]) for g in range(segments)], blocks)

    def some_tokens(step, states):
        states = list(states)
        for u in range(GROUP):
            token = step * GROUP + u
            at = pl.ds(pl.multiple_of(token * sub, sub), sub)
            sums = [None] * 4
            for n in range(modes):
                states[n] = states[n] * decay[n]
                sums[n % 4] = states[n] if sums[n % 4] is None else sums[n % 4] + states[n]
            added = (sums[0] + sums[1]) + (sums[2] + sums[3])
            carried[at, :] = local_ref[at, :] + jnp.where(token < limit, added, 0.0)
        return tuple(states)

    lax.fori_loop(
        0,
        steps // GROUP,
        some_tokens,
        tuple(mode_rows(by_mode, 1, n, sub) for n in range(modes)),
    )

    def finish(step, carry):
        first = step * part
        g, t = first // steps, first % steps
        rows = pl.ds(pl.multiple_of(first, part), part)
        for j in range(blocks):
            lanes = slice(j * LANES, (j + 1) * LANES)
            total = carried[pl.ds(t * sub + (g * blocks + j), part, stride=sub), :]
            out_ref[rows, lanes] = (front_ref[rows, lanes].astype(jnp.float32) * total).astype(
                out_ref.dtype
            )
        return carry

    lax.fori_loop(0, length // part, finish, 0)


def carry_shard(width, segments, limit, clear, ends, tables, base, front, local):
    length, channels = front.shape
    modes = tables[0].shape[0]
    blocks = width // LANES
    sub = segments * blocks
    specs = [SMEM, SMEM]
    specs += [whole_block(value.shape) for value in ends]
    specs += [pl.BlockSpec((modes, width), lambda g: (0, g)) for table in tables]
    specs.append(pl.BlockSpec((segments, modes, width), lambda g: (0, 0, g)))
    specs.append(pl.BlockSpec((length, width), lambda g: (0, g)))
    specs.append(pl.BlockSpec((length * blocks, LANES), lambda g: (g, 0)))
    return pl.pallas_call(
        functools.partial(carry_body, segments, len(ends)),
        grid=(channels // width,),
        in_specs=specs,
        out_specs=pl.BlockSpec((length, width), lambda g: (0, g)),
        out_shape=jax.ShapeDtypeStruct((length, channels), jnp.bfloat16),
        scratch_shapes=[
            pltpu.VMEM((2, modes * sub, LANES), jnp.float32),
            pltpu.VMEM((length * blocks, LANES), jnp.float32),
        ],
        compiler_params=pltpu.CompilerParams(vmem_limit_bytes=52 * 1024 * 1024),
        cost_estimate=pl.CostEstimate(
            flops=40 * length * channels, bytes_accessed=8 * length * channels, transcendentals=0
        ),
        name="carry_shard",
    )(limit, clear, *ends, *tables, base, front, local)


def on_device(arrived, landing, resets, short_taps, decay_rate, residues, skip_gain):
    shards, chans = lax.axis_size("seq"), lax.axis_size("chan")
    chan = lax.axis_index("chan")
    per_device = shards // chans
    length = resets.shape[0]
    channels = short_taps.shape[2]
    reach = short_taps.shape[1] - 1
    width = channels // CHUNKS
    segments = max(1, SUBLANES * LANES // width)

    def passed_along(value, by):
        return lax.ppermute(value, "seq", [(i, i + by) for i in range(shards - by)])

    place = chan.astype(jnp.int32)[None]
    slots = landing[0]
    final = jnp.argmax(slots == shards - 1)
    marks = resets.reshape(segments, -1)
    steps = marks.shape[1]
    limit = jnp.min(
        jnp.where(marks != 0, lax.broadcasted_iota(jnp.int32, marks.shape, 1), steps), axis=1
    )
    clear = (limit == steps).astype(jnp.float32)
    busy = jnp.sum(marks.reshape(segments, -1, GROUP), axis=(0, 2))
    decay = jnp.exp(-decay_rate)
    through = jnp.exp(-decay_rate * length)
    across = jnp.exp(-decay_rate * steps)
    gain = residues * jnp.sqrt(-jnp.expm1(-2.0 * decay_rate))
    skip = skip_gain[None]

    def across_plane(parts):
        return [
            lax.ppermute(part, "chan", [(c, c ^ d) for c in range(chans)])
            for d, part in enumerate(parts, start=1)
        ]

    def along_column(value):
        return lax.all_to_all(value, "seq", split_axis=0, concat_axis=0, tiled=True)

    own, *parts = cut_edges(place, arrived, per_device, reach, channels, chans)
    parts = [own, *across_plane(parts)]
    cuts = [cut_blocks(0, width, chans, place, arrived, [own])]
    edges = along_column(by_shard(place, parts, cuts[0]))
    last = lax.dynamic_index_in_dim(edges, final, axis=0, keepdims=False)
    before = passed_along(last, 1)

    scanned, ended = [], []
    for chunk in range(CHUNKS):
        blocks = across_plane(cuts[chunk])
        ready = [before] if chunk == 0 else ended[chunk - 2 : chunk - 1]
        if 0 < chunk < CHUNKS - 1:
            cuts.append(cut_blocks(chunk + 1, width, chans, place, arrived, [sent]))
            ready = [*ready, cuts[-1][0]]
        sent = slab_fronts(
            chunk, width, place, arrived, blocks, short_taps, per_device, ready
        )
        if chunk == 0:
            cuts.append(cut_blocks(1, width, chans, place, arrived, [sent]))
        scanned = scan_shard(
            chunk,
            width,
            segments,
            slots,
            resets,
            busy,
            clear,
            along_column(sent),
            edges,
            before,
            (short_taps, decay, gain, skip, across),
            scanned,
        )
        ended.append(scanned[3])
    front, local, base, _ = scanned
    ends = [passed_along(ended[-1], d) for d in range(1, shards)]
    return carry_shard(
        width, segments, limit, clear, ends, (through, across, decay, gain), base, front, local
    )


def solution(mesh):
    in_specs = (
        P(None, ("seq", "chan"), None),
        P("seq", None),
        P("seq"),
        P(None, None, "chan"),
        P(None, "chan"),
        P(None, "chan"),
        P("chan"),
    )
    out_specs = P("seq", "chan")
    return jax.shard_map(
        on_device, mesh=mesh, in_specs=in_specs, out_specs=out_specs, check_vma=False
    )
```

```python
import functools

import jax
import jax.numpy as jnp
from jax import lax
from jax.experimental import pallas as pl
from jax.experimental.pallas import tpu as pltpu
from jax.sharding import PartitionSpec as P

LANES = 128
SUBLANES = 8
GROUP = 16
CHUNKS = 4
VMEM_BYTES = 50 * 1024 * 1024

SMEM = pl.BlockSpec(memory_space=pltpu.SMEM)
VMEM = pl.BlockSpec(memory_space=pltpu.VMEM)
ANY = pl.BlockSpec(memory_space=pl.ANY)
PARAMS = pltpu.CompilerParams(vmem_limit_bytes=VMEM_BYTES)


def columns_of(table, chunk, width):
    lead = table.shape[:-1]
    return pl.BlockSpec((*lead, width), lambda g: (0,) * len(lead) + (chunk,))


def column_start(place_ref, d, chunk, width):
    return pl.multiple_of(((place_ref[0] ^ d) * CHUNKS + chunk) * width, LANES)


def cut_blocks(chunk, width, chans, place, arrived, later):

    def body(place_ref, arrived_ref, *refs):
        outs, sems = refs[len(later) : -1], refs[-1]
        copies = []
        for d, out in enumerate(outs, start=1):
            start = column_start(place_ref, d, chunk, width)
            copies.append(
                pltpu.make_async_copy(
                    arrived_ref.at[:, :, pl.ds(start, width)], out, sems.at[d - 1]
                )
            )
        for copy in copies:
            copy.start()
        for copy in copies:
            copy.wait()

    shape = jax.ShapeDtypeStruct((*arrived.shape[:2], width), arrived.dtype)
    return pl.pallas_call(
        body,
        in_specs=[SMEM, ANY] + [ANY] * len(later),
        out_specs=[VMEM] * (chans - 1),
        out_shape=[shape] * (chans - 1),
        scratch_shapes=[pltpu.SemaphoreType.DMA((chans - 1,))],
        compiler_params=PARAMS,
        name="cut_blocks",
    )(place, arrived, *later)


def shift_window(rows, start, count):
    return lax.slice_in_dim(rows, start, start + count, axis=0)


def cut_edges(place, arrived, per_device, reach, channels, chans):
    slab = arrived.shape[1] // per_device

    def body(place_ref, arrived_ref, *refs):
        outs, (tails, heads, sems) = refs[:chans], refs[chans:]
        copies = []
        for d in range(chans):
            start = pl.multiple_of((place_ref[0] ^ d) * channels, LANES)
            here = pl.ds(start, channels)
            for i in range(per_device):
                at = len(copies)
                copies.append(
                    pltpu.make_async_copy(
                        arrived_ref.at[:, pl.ds((i + 1) * slab - 16, 16), here],
                        tails.at[d, i],
                        sems.at[at],
                    )
                )
                copies.append(
                    pltpu.make_async_copy(
                        arrived_ref.at[2, pl.ds(i * slab, 16), here],
                        heads.at[d, i],
                        sems.at[at + 1],
                    )
                )
        for copy in copies:
            copy.start()
        for copy in copies:
            copy.wait()

        for d in range(chans):

            def one_block(block, carry, d=d):
                lanes = pl.ds(pl.multiple_of(block * LANES, LANES), LANES)
                for i in range(per_device):
                    parts = [
                        tails[d, i, k, :, lanes].astype(jnp.float32)[16 - reach :] for k in range(3)
                    ]
                    parts.append(heads[d, i, :, lanes].astype(jnp.float32)[:reach])
                    outs[d][i, :, lanes] = jnp.concatenate(parts, axis=0).astype(arrived.dtype)
                return carry

            lax.fori_loop(0, channels // LANES, one_block, 0)

    shape = jax.ShapeDtypeStruct((per_device, 4 * reach, channels), arrived.dtype)
    return pl.pallas_call(
        body,
        in_specs=[SMEM, ANY],
        out_specs=[VMEM] * chans,
        out_shape=[shape] * chans,
        scratch_shapes=[
            pltpu.VMEM((chans, per_device, 3, 16, channels), arrived.dtype),
            pltpu.VMEM((chans, per_device, 16, channels), arrived.dtype),
            pltpu.SemaphoreType.DMA((2 * chans * per_device,)),
        ],
        compiler_params=PARAMS,
        name="cut_edges",
    )(place, arrived)


def by_shard(place, parts, later):
    count = len(parts)
    per_device, rows, channels = parts[0].shape

    def body(place_ref, *refs):
        part_refs, (out_ref, sems) = refs[:count], refs[-2:]
        copies = [
            pltpu.make_async_copy(
                part_refs[d],
                out_ref.at[pl.ds((place_ref[0] ^ d) * per_device, per_device)],
                sems.at[d],
            )
            for d in range(count)
        ]
        for copy in copies:
            copy.start()
        for copy in copies:
            copy.wait()

    return pl.pallas_call(
        body,
        in_specs=[SMEM] + [ANY] * (count + len(later)),
        out_specs=VMEM,
        out_shape=jax.ShapeDtypeStruct((count * per_device, rows, channels), parts[0].dtype),
        scratch_shapes=[pltpu.SemaphoreType.DMA((count,))],
        compiler_params=PARAMS,
        name="by_shard",
    )(place, *parts, *later)


def in_place(value, later):
    def body(value_ref, later_ref, out_ref):
        pass

    return pl.pallas_call(
        body,
        in_specs=[ANY, ANY],
        out_specs=ANY,
        out_shape=jax.ShapeDtypeStruct(value.shape, value.dtype),
        input_output_aliases={0: 0},
        compiler_params=PARAMS,
        name="in_place",
    )(value, later)


def front_body(chunk, count, place_ref, arrived_ref, *refs):
    block_refs = refs[: count - 1]
    taps_ref, out_ref, held, padded, sems = refs[-5:]
    shards, _, width = out_ref.shape
    per_device = shards // count
    slab = held.shape[2] // per_device
    taps = taps_ref.shape[1]
    reach = taps - 1
    blocks = width // LANES
    row_ids = lax.broadcasted_iota(jnp.int32, (slab, LANES), 0)
    sources = [arrived_ref.at[:, :, pl.ds(column_start(place_ref, 0, chunk, width), width)]]
    sources += block_refs
    copies = [pltpu.make_async_copy(sources[d], held.at[d], sems.at[d]) for d in range(count)]
    for copy in copies:
        copy.start()
    for k in range(3):
        padded[k, :8, :] = jnp.zeros((8, LANES), jnp.float32)
    for d in range(count):
        copies[d].wait()

        def one_block(step, carry, d=d):
            i, block = step // blocks, step % blocks
            lanes = pl.ds(pl.multiple_of(block * LANES, LANES), LANES)
            own = pl.ds(pl.multiple_of(i * slab, slab), slab)
            shard = (place_ref[0] ^ d) * per_device + i

            def conv(k):
                rows = held[d, k, own, lanes].astype(jnp.float32)
                padded[k, 8:, :] = rows
                total = taps_ref[k, 0:1, lanes] * rows
                for j in range(1, taps):
                    total = total + taps_ref[k, j : j + 1, lanes] * padded[k, 8 - j : 8 - j + slab, :]
                return total

            front = conv(0)
            key = conv(1)
            value = conv(2)
            gate = jnp.where(row_ids < reach, key, key * value)
            out_ref[shard, :slab, lanes] = front.astype(out_ref.dtype)
            out_ref[shard, slab:, lanes] = gate.astype(out_ref.dtype)
            return carry

        lax.fori_loop(0, per_device * blocks, one_block, 0)


def slab_fronts(chunk, width, place, arrived, blocks, taps, per_device, after):
    count = len(blocks) + 1
    rows = arrived.shape[1]
    shape = (count * per_device, 2 * (rows // per_device), width)
    return pl.pallas_call(
        functools.partial(front_body, chunk, count),
        grid=(1,),
        in_specs=[SMEM] + [ANY] * (count + len(after)) + [columns_of(taps, chunk, width)],
        out_specs=pl.BlockSpec(shape, lambda g: (0, 0, 0)),
        out_shape=jax.ShapeDtypeStruct(shape, arrived.dtype),
        scratch_shapes=[
            pltpu.VMEM((count, 3, rows, width), arrived.dtype),
            pltpu.VMEM((3, rows // per_device + 8, LANES), jnp.float32),
            pltpu.SemaphoreType.DMA((count,)),
        ],
        compiler_params=PARAMS,
        cost_estimate=pl.CostEstimate(
            flops=60 * count * rows * width,
            bytes_accessed=10 * count * rows * width,
            transcendentals=0,
        ),
        name="slab_fronts",
    )(place, arrived, *blocks, *after, taps)


def spread(values, blocks):
    if len(values) == 1:
        return values[0]
    ids = lax.broadcasted_iota(jnp.int32, (len(values) * blocks, LANES), 0)
    out = jnp.full(ids.shape, values[-1])
    for g in range(len(values) - 2, -1, -1):
        out = jnp.where(ids < (g + 1) * blocks, values[g], out)
    return out


def mode_rows(ref, table, n, sub):
    return ref[table, n * sub : (n + 1) * sub, :]


def scan_body(chunk, segments, shared, *refs):
    slots_ref, resets_ref, busy_ref, clear_ref, slab_ref, edge_ref, before_ref = refs[:7]
    taps_ref, decay_ref, gain_ref, skip_ref, across_ref = refs[7:12]
    earlier_refs = refs[12 : 12 + (shared > 0)]
    front_ref, local_ref, base_ref, ended_ref = refs[12 + shared : 16 + shared]
    slabs, edges, wide, by_mode, sems = refs[16 + shared :]
    count, rows, width = slabs.shape
    taps = taps_ref.shape[1]
    reach = taps - 1
    slab = rows // 2
    modes = decay_ref.shape[0]
    blocks = width // LANES
    sub = segments * blocks
    steps = count * slab // segments

    here = pl.ds(chunk * width, width)
    copies = [pltpu.make_async_copy(before_ref.at[:, here], edges.at[0], sems.at[2 * count])]
    for m in range(count):
        slot = slots_ref[m]
        copies.append(pltpu.make_async_copy(slab_ref.at[m], slabs.at[slot], sems.at[m]))
        copies.append(
            pltpu.make_async_copy(
                edge_ref.at[m, :, here], edges.at[slot + 1], sems.at[count + m]
            )
        )
    for copy in copies:
        copy.start()
    for g in range(segments):
        for j in range(blocks):
            lanes = slice(j * LANES, (j + 1) * LANES)
            at = g * blocks + j
            by_mode[0, pl.ds(at, modes, stride=sub), :] = decay_ref[:, lanes]
            by_mode[1, pl.ds(at, modes, stride=sub), :] = gain_ref[:, lanes]
            by_mode[2, at : at + 1, :] = skip_ref[:, lanes]
    for ref in earlier_refs:
        ended_ref[:, : chunk * width] = ref[:, : chunk * width]
    for copy in copies:
        copy.wait()

    row_ids = lax.broadcasted_iota(jnp.int32, (slab, LANES), 0)
    blank = jnp.zeros((16 - reach, LANES), jnp.float32)

    def one_slot(slot, carry):
        first = slot * slab
        g, t = first // steps, first % steps
        for j in range(blocks):
            lanes = slice(j * LANES, (j + 1) * LANES)
            edge = edges[slot, :, lanes].astype(jnp.float32)
            own = edges[slot + 1, :, lanes].astype(jnp.float32)

            def from_rows(k, rows, least):
                total = jnp.zeros((8, LANES), jnp.float32)
                for tap in range(least, taps):
                    total = total + taps_ref[k, tap : tap + 1, lanes] * shift_window(
                        rows, reach - tap, 8
                    )
                return total

            def tail(k):
                return edge[k * reach : (k + 1) * reach]

            add_front = from_rows(0, jnp.concatenate([tail(0), blank], axis=0), 1)
            add_key = from_rows(1, jnp.concatenate([tail(1), blank], axis=0), 1)
            value = from_rows(
                2, jnp.concatenate([tail(2), own[3 * reach :], blank[reach:]], axis=0), 0
            )
            starts = row_ids[:8] < reach
            front = slabs[slot, :slab, lanes].astype(jnp.float32)
            gate = slabs[slot, slab:, lanes].astype(jnp.float32)
            front_start = jnp.where(starts, front[:8] + add_front, front[:8])
            gate_start = ((gate[:8] + add_key) * value).astype(jnp.bfloat16)
            gate_start = jnp.where(starts, gate_start.astype(jnp.float32), gate[:8])
            front = jnp.concatenate([front_start, front[8:]], axis=0)
            gate = jnp.concatenate([gate_start, gate[8:]], axis=0)
            base = pl.multiple_of(first, slab)
            front_ref[pl.ds(base, slab), lanes] = front.astype(front_ref.dtype)
            wide[pl.ds(t * sub + (g * blocks + j), slab, stride=sub), :] = gate

        return carry

    lax.fori_loop(0, count, one_slot, 0)

    decay = [mode_rows(by_mode, 0, n, sub) for n in range(modes)]
    gain = [mode_rows(by_mode, 1, n, sub) for n in range(modes)]
    skip = by_mode[2, 0:sub, :]

    def tokens(step, states, with_resets):
        states = list(states)
        for u in range(GROUP):
            token = step * GROUP + u
            at = pl.ds(pl.multiple_of(token * sub, sub), sub)
            if with_resets:
                hold = spread(
                    [
                        jnp.where(resets_ref[g * steps + token] == 0, 1.0, 0.0)
                        for g in range(segments)
                    ],
                    blocks,
                )
                states = [state * hold for state in states]
            gate = wide[at, :]
            sums = [skip * gate, None]
            for n in range(modes):
                states[n] = states[n] * decay[n] + gate
                term = gain[n] * states[n]
                sums[n % 2] = term if sums[n % 2] is None else sums[n % 2] + term
            local_ref[at, :] = sums[0] + sums[1]
        return tuple(states)

    def some_tokens(step, states):
        return lax.cond(
            busy_ref[step] == 0,
            lambda held: tokens(step, held, False),
            lambda held: tokens(step, held, True),
            states,
        )

    zero = jnp.zeros((sub, LANES), jnp.float32)
    states = lax.fori_loop(0, steps // GROUP, some_tokens, (zero,) * modes)
    for n in range(modes):
        by_mode[0, n * sub : (n + 1) * sub, :] = states[n]
    open_shard = clear_ref[0]
    for g in range(1, segments):
        open_shard = open_shard * clear_ref[g]
    for j in range(blocks):
        lanes = slice(j * LANES, (j + 1) * LANES)
        entering = jnp.zeros((modes, LANES), jnp.float32)
        for g in range(segments):
            base_ref[g, :, lanes] = entering
            ended = by_mode[0, pl.ds(g * blocks + j, modes, stride=sub), :]
            entering = ended + across_ref[:, lanes] * clear_ref[g] * entering
        ended_ref[:, chunk * width + j * LANES : chunk * width + (j + 1) * LANES] = (
            entering.astype(ended_ref.dtype)
        )
    ended_ref[:, (chunk + 1) * width :] = jnp.full(
        (modes, LANES), open_shard, jnp.float32
    ).astype(ended_ref.dtype)


def whole_block(shape):
    return pl.BlockSpec(shape, lambda g: (0,) * len(shape))


def scan_shard(
    chunk, width, segments, slots, resets, busy, clear, slabs, edges, before, tables, earlier
):
    count, rows, _ = slabs.shape
    length = resets.shape[0]
    modes, channels = tables[1].shape
    blocks = width // LANES
    sub = segments * blocks
    outs = [
        jax.ShapeDtypeStruct((length, channels), jnp.bfloat16),
        jax.ShapeDtypeStruct((length * channels // LANES, LANES), jnp.float32),
        jax.ShapeDtypeStruct((segments, modes, channels), jnp.float32),
        jax.ShapeDtypeStruct((modes, (chunk + 1) * width + LANES), jnp.bfloat16),
    ]
    shared = [*earlier[3:], *earlier[:3]]
    first = 7 + len(tables) + 1
    return pl.pallas_call(
        functools.partial(scan_body, chunk, segments, len(shared)),
        grid=(1,),
        in_specs=[SMEM] * 4 + [ANY] * 3
        + [columns_of(table, chunk, width) for table in tables]
        + [whole_block(value.shape) for value in shared[:1]]
        + [ANY] * len(shared[1:]),
        out_specs=[
            columns_of(outs[0], chunk, width),
            pl.BlockSpec((length * blocks, LANES), lambda g: (chunk, 0)),
            columns_of(outs[2], chunk, width),
            whole_block(outs[3].shape),
        ],
        out_shape=outs,
        input_output_aliases={first + i: i for i in range(len(shared[1:]))},
        scratch_shapes=[
            pltpu.VMEM((count, rows, width), jnp.bfloat16),
            pltpu.VMEM((count + 1, edges.shape[1], width), jnp.bfloat16),
            pltpu.VMEM((length * blocks, LANES), jnp.float32),
            pltpu.VMEM((3, modes * sub, LANES), jnp.float32),
            pltpu.SemaphoreType.DMA((2 * count + 1,)),
        ],
        compiler_params=PARAMS,
        cost_estimate=pl.CostEstimate(
            flops=100 * length * width, bytes_accessed=10 * length * width, transcendentals=0
        ),
        name="scan_shard",
    )(slots, resets, busy, clear, slabs, edges, before, *tables, *shared)


def carry_body(segments, count, *refs):
    limit_ref, clear_ref = refs[:2]
    end_refs = refs[2 : 2 + count]
    through_ref, across_ref, decay_ref, gain_ref = refs[2 + count : 6 + count]
    base_ref, front_ref, local_ref = refs[6 + count : 9 + count]
    out_ref, by_mode, carried = refs[-3:]
    modes, width = decay_ref.shape
    length = front_ref.shape[0]
    blocks = width // LANES
    sub = segments * blocks
    steps = length // segments
    part = min(64, steps)
    for j in range(blocks):
        lanes = slice(j * LANES, (j + 1) * LANES)
        here = pl.ds(pl.multiple_of(pl.program_id(0) * width + j * LANES, LANES), LANES)
        entering = jnp.zeros((modes, LANES), jnp.float32)
        for ref in reversed(end_refs):
            is_open = ref[:, ref.shape[1] - LANES :].astype(jnp.float32)
            entering = ref[:, here].astype(jnp.float32) + (
                through_ref[:, lanes] * is_open * entering
            )
        for g in range(segments):
            at = pl.ds(g * blocks + j, modes, stride=sub)
            by_mode[0, at, :] = decay_ref[:, lanes]
            by_mode[1, at, :] = gain_ref[:, lanes] * (base_ref[g, :, lanes] + entering)
            entering = entering * across_ref[:, lanes] * clear_ref[g]
    decay = [mode_rows(by_mode, 0, n, sub) for n in range(modes)]
    limit = spread([jnp.full((sub, LANES), limit_ref[g]) for g in range(segments)], blocks)

    def some_tokens(step, states):
        states = list(states)
        for u in range(GROUP):
            token = step * GROUP + u
            at = pl.ds(pl.multiple_of(token * sub, sub), sub)
            sums = [None] * 4
            for n in range(modes):
                states[n] = states[n] * decay[n]
                sums[n % 4] = states[n] if sums[n % 4] is None else sums[n % 4] + states[n]
            added = (sums[0] + sums[1]) + (sums[2] + sums[3])
            carried[at, :] = local_ref[at, :] + jnp.where(token < limit, added, 0.0)
        return tuple(states)

    lax.fori_loop(
        0,
        steps // GROUP,
        some_tokens,
        tuple(mode_rows(by_mode, 1, n, sub) for n in range(modes)),
    )

    def finish(step, carry):
        first = step * part
        g, t = first // steps, first % steps
        rows = pl.ds(pl.multiple_of(first, part), part)
        for j in range(blocks):
            lanes = slice(j * LANES, (j + 1) * LANES)
            total = carried[pl.ds(t * sub + (g * blocks + j), part, stride=sub), :]
            out_ref[rows, lanes] = (front_ref[rows, lanes].astype(jnp.float32) * total).astype(
                out_ref.dtype
            )
        return carry

    lax.fori_loop(0, length // part, finish, 0)


def carry_shard(width, segments, limit, clear, ends, tables, base, front, local):
    length, channels = front.shape
    modes = tables[0].shape[0]
    blocks = width // LANES
    sub = segments * blocks
    specs = [SMEM, SMEM]
    specs += [whole_block(value.shape) for value in ends]
    specs += [pl.BlockSpec((modes, width), lambda g: (0, g)) for table in tables]
    specs.append(pl.BlockSpec((segments, modes, width), lambda g: (0, 0, g)))
    specs.append(pl.BlockSpec((length, width), lambda g: (0, g)))
    specs.append(pl.BlockSpec((length * blocks, LANES), lambda g: (g, 0)))
    return pl.pallas_call(
        functools.partial(carry_body, segments, len(ends)),
        grid=(channels // width,),
        in_specs=specs,
        out_specs=pl.BlockSpec((length, width), lambda g: (0, g)),
        out_shape=jax.ShapeDtypeStruct((length, channels), jnp.bfloat16),
        scratch_shapes=[
            pltpu.VMEM((2, modes * sub, LANES), jnp.float32),
            pltpu.VMEM((length * blocks, LANES), jnp.float32),
        ],
        compiler_params=pltpu.CompilerParams(vmem_limit_bytes=52 * 1024 * 1024),
        cost_estimate=pl.CostEstimate(
            flops=40 * length * channels, bytes_accessed=8 * length * channels, transcendentals=0
        ),
        name="carry_shard",
    )(limit, clear, *ends, *tables, base, front, local)


def on_device(arrived, landing, resets, short_taps, decay_rate, residues, skip_gain):
    shards, chans = lax.axis_size("seq"), lax.axis_size("chan")
    chan = lax.axis_index("chan")
    per_device = shards // chans
    length = resets.shape[0]
    channels = short_taps.shape[2]
    reach = short_taps.shape[1] - 1
    width = channels // CHUNKS
    segments = max(1, SUBLANES * LANES // width)

    def passed_along(value, by):
        return lax.ppermute(value, "seq", [(i, i + by) for i in range(shards - by)])

    place = chan.astype(jnp.int32)[None]
    slots = landing[0]
    final = jnp.argmax(slots == shards - 1)
    marks = resets.reshape(segments, -1)
    steps = marks.shape[1]
    limit = jnp.min(
        jnp.where(marks != 0, lax.broadcasted_iota(jnp.int32, marks.shape, 1), steps), axis=1
    )
    clear = (limit == steps).astype(jnp.float32)
    busy = jnp.sum(marks.reshape(segments, -1, GROUP), axis=(0, 2))
    decay = jnp.exp(-decay_rate)
    through = jnp.exp(-decay_rate * length)
    across = jnp.exp(-decay_rate * steps)
    gain = residues * jnp.sqrt(-jnp.expm1(-2.0 * decay_rate))
    skip = skip_gain[None]

    def across_plane(parts):
        return [
            lax.ppermute(part, "chan", [(c, c ^ d) for c in range(chans)])
            for d, part in enumerate(parts, start=1)
        ]

    def along_column(value):
        return lax.all_to_all(value, "seq", split_axis=0, concat_axis=0, tiled=True)

    own, *parts = cut_edges(place, arrived, per_device, reach, channels, chans)
    parts = [own, *across_plane(parts)]
    cuts = [cut_blocks(0, width, chans, place, arrived, [own])]
    edges = along_column(by_shard(place, parts, cuts[0]))
    last = lax.dynamic_index_in_dim(edges, final, axis=0, keepdims=False)
    before = passed_along(last, 1)

    scanned, ended = [], []
    for chunk in range(CHUNKS):
        blocks = across_plane(cuts[chunk])
        ready = []
        if 0 < chunk < CHUNKS - 1:
            cuts.append(cut_blocks(chunk + 1, width, chans, place, arrived, [sent]))
            ready = [*ready, cuts[-1][0]]
        sent = slab_fronts(
            chunk, width, place, arrived, blocks, short_taps, per_device, ready
        )
        if chunk == CHUNKS - 1:
            sent = in_place(sent, before)
        if chunk == 0:
            cuts.append(cut_blocks(1, width, chans, place, arrived, [sent]))
        scanned = scan_shard(
            chunk,
            width,
            segments,
            slots,
            resets,
            busy,
            clear,
            along_column(sent),
            edges,
            before,
            (short_taps, decay, gain, skip, across),
            scanned,
        )
        ended.append(scanned[3])
    front, local, base, _ = scanned
    ends = [passed_along(ended[-1], d) for d in range(1, shards)]
    return carry_shard(
        width, segments, limit, clear, ends, (through, across, decay, gain), base, front, local
    )


def solution(mesh):
    in_specs = (
        P(None, ("seq", "chan"), None),
        P("seq", None),
        P("seq"),
        P(None, None, "chan"),
        P(None, "chan"),
        P(None, "chan"),
        P("chan"),
    )
    out_specs = P("seq", "chan")
    return jax.shard_map(
        on_device, mesh=mesh, in_specs=in_specs, out_specs=out_specs, check_vma=False
    )
```

```python
import functools

import jax
import jax.numpy as jnp
from jax import lax
from jax.experimental import pallas as pl
from jax.experimental.pallas import tpu as pltpu
from jax.sharding import PartitionSpec as P

LANES = 128
SUBLANES = 8
GROUP = 16
CHUNKS = 4
VMEM_BYTES = 50 * 1024 * 1024

SMEM = pl.BlockSpec(memory_space=pltpu.SMEM)
VMEM = pl.BlockSpec(memory_space=pltpu.VMEM)
ANY = pl.BlockSpec(memory_space=pl.ANY)
PARAMS = pltpu.CompilerParams(vmem_limit_bytes=VMEM_BYTES)


def columns_of(table, chunk, width):
    lead = table.shape[:-1]
    return pl.BlockSpec((*lead, width), lambda g: (0,) * len(lead) + (chunk,))


def column_start(place_ref, d, chunk, width):
    return pl.multiple_of(((place_ref[0] ^ d) * CHUNKS + chunk) * width, LANES)


def cut_blocks(chunk, width, chans, place, arrived, later):

    def body(place_ref, arrived_ref, *refs):
        outs, sems = refs[len(later) : -1], refs[-1]
        copies = []
        for d, out in enumerate(outs, start=1):
            start = column_start(place_ref, d, chunk, width)
            copies.append(
                pltpu.make_async_copy(
                    arrived_ref.at[:, :, pl.ds(start, width)], out, sems.at[d - 1]
                )
            )
        for copy in copies:
            copy.start()
        for copy in copies:
            copy.wait()

    shape = jax.ShapeDtypeStruct((*arrived.shape[:2], width), arrived.dtype)
    return pl.pallas_call(
        body,
        in_specs=[SMEM, ANY] + [ANY] * len(later),
        out_specs=[VMEM] * (chans - 1),
        out_shape=[shape] * (chans - 1),
        scratch_shapes=[pltpu.SemaphoreType.DMA((chans - 1,))],
        compiler_params=PARAMS,
        name="cut_blocks",
    )(place, arrived, *later)


def shift_window(rows, start, count):
    return lax.slice_in_dim(rows, start, start + count, axis=0)


def cut_edges(place, arrived, per_device, reach, channels, chans):
    slab = arrived.shape[1] // per_device

    def body(place_ref, arrived_ref, *refs):
        outs, (tails, heads, sems) = refs[:chans], refs[chans:]
        copies = []
        for d in range(chans):
            start = pl.multiple_of((place_ref[0] ^ d) * channels, LANES)
            here = pl.ds(start, channels)
            for i in range(per_device):
                at = len(copies)
                copies.append(
                    pltpu.make_async_copy(
                        arrived_ref.at[:, pl.ds((i + 1) * slab - 16, 16), here],
                        tails.at[d, i],
                        sems.at[at],
                    )
                )
                copies.append(
                    pltpu.make_async_copy(
                        arrived_ref.at[2, pl.ds(i * slab, 16), here],
                        heads.at[d, i],
                        sems.at[at + 1],
                    )
                )
        for copy in copies:
            copy.start()
        for copy in copies:
            copy.wait()

        for d in range(chans):

            def one_block(block, carry, d=d):
                lanes = pl.ds(pl.multiple_of(block * LANES, LANES), LANES)
                for i in range(per_device):
                    parts = [
                        tails[d, i, k, :, lanes].astype(jnp.float32)[16 - reach :] for k in range(3)
                    ]
                    parts.append(heads[d, i, :, lanes].astype(jnp.float32)[:reach])
                    outs[d][i, :, lanes] = jnp.concatenate(parts, axis=0).astype(arrived.dtype)
                return carry

            lax.fori_loop(0, channels // LANES, one_block, 0)

    shape = jax.ShapeDtypeStruct((per_device, 4 * reach, channels), arrived.dtype)
    return pl.pallas_call(
        body,
        in_specs=[SMEM, ANY],
        out_specs=[VMEM] * chans,
        out_shape=[shape] * chans,
        scratch_shapes=[
            pltpu.VMEM((chans, per_device, 3, 16, channels), arrived.dtype),
            pltpu.VMEM((chans, per_device, 16, channels), arrived.dtype),
            pltpu.SemaphoreType.DMA((2 * chans * per_device,)),
        ],
        compiler_params=PARAMS,
        name="cut_edges",
    )(place, arrived)


def by_shard(place, parts, later):
    count = len(parts)
    per_device, rows, channels = parts[0].shape

    def body(place_ref, *refs):
        part_refs, (out_ref, sems) = refs[:count], refs[-2:]
        copies = [
            pltpu.make_async_copy(
                part_refs[d],
                out_ref.at[pl.ds((place_ref[0] ^ d) * per_device, per_device)],
                sems.at[d],
            )
            for d in range(count)
        ]
        for copy in copies:
            copy.start()
        for copy in copies:
            copy.wait()

    return pl.pallas_call(
        body,
        in_specs=[SMEM] + [ANY] * (count + len(later)),
        out_specs=VMEM,
        out_shape=jax.ShapeDtypeStruct((count * per_device, rows, channels), parts[0].dtype),
        scratch_shapes=[pltpu.SemaphoreType.DMA((count,))],
        compiler_params=PARAMS,
        name="by_shard",
    )(place, *parts, *later)


def in_place(value, later):
    def body(value_ref, later_ref, out_ref):
        pass

    return pl.pallas_call(
        body,
        in_specs=[ANY, ANY],
        out_specs=ANY,
        out_shape=jax.ShapeDtypeStruct(value.shape, value.dtype),
        input_output_aliases={0: 0},
        compiler_params=PARAMS,
        name="in_place",
    )(value, later)


def front_body(chunk, count, place_ref, arrived_ref, *refs):
    block_refs = refs[: count - 1]
    taps_ref, out_ref, held, padded, sems = refs[-5:]
    shards, _, width = out_ref.shape
    per_device = shards // count
    slab = held.shape[2] // per_device
    taps = taps_ref.shape[1]
    reach = taps - 1
    blocks = width // LANES
    row_ids = lax.broadcasted_iota(jnp.int32, (slab, LANES), 0)
    sources = [arrived_ref.at[:, :, pl.ds(column_start(place_ref, 0, chunk, width), width)]]
    sources += block_refs
    copies = [pltpu.make_async_copy(sources[d], held.at[d], sems.at[d]) for d in range(count)]
    for copy in copies:
        copy.start()
    for k in range(3):
        padded[k, :8, :] = jnp.zeros((8, LANES), jnp.float32)
    for d in range(count):
        copies[d].wait()

        def one_block(step, carry, d=d):
            i, block = step // blocks, step % blocks
            lanes = pl.ds(pl.multiple_of(block * LANES, LANES), LANES)
            own = pl.ds(pl.multiple_of(i * slab, slab), slab)
            shard = (place_ref[0] ^ d) * per_device + i

            def conv(k):
                rows = held[d, k, own, lanes].astype(jnp.float32)
                padded[k, 8:, :] = rows
                total = taps_ref[k, 0:1, lanes] * rows
                for j in range(1, taps):
                    total = total + taps_ref[k, j : j + 1, lanes] * padded[k, 8 - j : 8 - j + slab, :]
                return total

            front = conv(0)
            key = conv(1)
            value = conv(2)
            gate = jnp.where(row_ids < reach, key, key * value)
            out_ref[shard, :slab, lanes] = front.astype(out_ref.dtype)
            out_ref[shard, slab:, lanes] = gate.astype(out_ref.dtype)
            return carry

        lax.fori_loop(0, per_device * blocks, one_block, 0, unroll=2)


def slab_fronts(chunk, width, place, arrived, blocks, taps, per_device, after):
    count = len(blocks) + 1
    rows = arrived.shape[1]
    shape = (count * per_device, 2 * (rows // per_device), width)
    return pl.pallas_call(
        functools.partial(front_body, chunk, count),
        grid=(1,),
        in_specs=[SMEM] + [ANY] * (count + len(after)) + [columns_of(taps, chunk, width)],
        out_specs=pl.BlockSpec(shape, lambda g: (0, 0, 0)),
        out_shape=jax.ShapeDtypeStruct(shape, arrived.dtype),
        scratch_shapes=[
            pltpu.VMEM((count, 3, rows, width), arrived.dtype),
            pltpu.VMEM((3, rows // per_device + 8, LANES), jnp.float32),
            pltpu.SemaphoreType.DMA((count,)),
        ],
        compiler_params=PARAMS,
        cost_estimate=pl.CostEstimate(
            flops=60 * count * rows * width,
            bytes_accessed=10 * count * rows * width,
            transcendentals=0,
        ),
        name="slab_fronts",
    )(place, arrived, *blocks, *after, taps)


def spread(values, blocks):
    if len(values) == 1:
        return values[0]
    ids = lax.broadcasted_iota(jnp.int32, (len(values) * blocks, LANES), 0)
    out = jnp.full(ids.shape, values[-1])
    for g in range(len(values) - 2, -1, -1):
        out = jnp.where(ids < (g + 1) * blocks, values[g], out)
    return out


def mode_rows(ref, table, n, sub):
    return ref[table, n * sub : (n + 1) * sub, :]


def scan_body(chunk, segments, shared, *refs):
    slots_ref, resets_ref, busy_ref, clear_ref, slab_ref, edge_ref, before_ref = refs[:7]
    taps_ref, decay_ref, gain_ref, skip_ref, across_ref = refs[7:12]
    earlier_refs = refs[12 : 12 + (shared > 0)]
    front_ref, local_ref, base_ref, ended_ref = refs[12 + shared : 16 + shared]
    slabs, edges, wide, by_mode, sems = refs[16 + shared :]
    count, rows, width = slabs.shape
    taps = taps_ref.shape[1]
    reach = taps - 1
    slab = rows // 2
    modes = decay_ref.shape[0]
    blocks = width // LANES
    sub = segments * blocks
    steps = count * slab // segments

    here = pl.ds(chunk * width, width)
    copies = [pltpu.make_async_copy(before_ref.at[:, here], edges.at[0], sems.at[2 * count])]
    for m in range(count):
        slot = slots_ref[m]
        copies.append(pltpu.make_async_copy(slab_ref.at[m], slabs.at[slot], sems.at[m]))
        copies.append(
            pltpu.make_async_copy(
                edge_ref.at[m, :, here], edges.at[slot + 1], sems.at[count + m]
            )
        )
    for copy in copies:
        copy.start()
    for g in range(segments):
        for j in range(blocks):
            lanes = slice(j * LANES, (j + 1) * LANES)
            at = g * blocks + j
            by_mode[0, pl.ds(at, modes, stride=sub), :] = decay_ref[:, lanes]
            by_mode[1, pl.ds(at, modes, stride=sub), :] = gain_ref[:, lanes]
            by_mode[2, at : at + 1, :] = skip_ref[:, lanes]
    for ref in earlier_refs:
        ended_ref[:, : chunk * width] = ref[:, : chunk * width]
    for copy in copies:
        copy.wait()

    row_ids = lax.broadcasted_iota(jnp.int32, (slab, LANES), 0)
    blank = jnp.zeros((16 - reach, LANES), jnp.float32)

    def one_slot(slot, carry):
        first = slot * slab
        g, t = first // steps, first % steps
        for j in range(blocks):
            lanes = slice(j * LANES, (j + 1) * LANES)
            edge = edges[slot, :, lanes].astype(jnp.float32)
            own = edges[slot + 1, :, lanes].astype(jnp.float32)

            def from_rows(k, rows, least):
                total = jnp.zeros((8, LANES), jnp.float32)
                for tap in range(least, taps):
                    total = total + taps_ref[k, tap : tap + 1, lanes] * shift_window(
                        rows, reach - tap, 8
                    )
                return total

            def tail(k):
                return edge[k * reach : (k + 1) * reach]

            add_front = from_rows(0, jnp.concatenate([tail(0), blank], axis=0), 1)
            add_key = from_rows(1, jnp.concatenate([tail(1), blank], axis=0), 1)
            value = from_rows(
                2, jnp.concatenate([tail(2), own[3 * reach :], blank[reach:]], axis=0), 0
            )
            starts = row_ids[:8] < reach
            front = slabs[slot, :slab, lanes].astype(jnp.float32)
            gate = slabs[slot, slab:, lanes].astype(jnp.float32)
            front_start = jnp.where(starts, front[:8] + add_front, front[:8])
            gate_start = ((gate[:8] + add_key) * value).astype(jnp.bfloat16)
            gate_start = jnp.where(starts, gate_start.astype(jnp.float32), gate[:8])
            front = jnp.concatenate([front_start, front[8:]], axis=0)
            gate = jnp.concatenate([gate_start, gate[8:]], axis=0)
            base = pl.multiple_of(first, slab)
            front_ref[pl.ds(base, slab), lanes] = front.astype(front_ref.dtype)
            wide[pl.ds(t * sub + (g * blocks + j), slab, stride=sub), :] = gate

        return carry

    lax.fori_loop(0, count, one_slot, 0)

    decay = [mode_rows(by_mode, 0, n, sub) for n in range(modes)]
    gain = [mode_rows(by_mode, 1, n, sub) for n in range(modes)]
    skip = by_mode[2, 0:sub, :]

    def tokens(step, states, with_resets):
        states = list(states)
        for u in range(GROUP):
            token = step * GROUP + u
            at = pl.ds(pl.multiple_of(token * sub, sub), sub)
            if with_resets:
                hold = spread(
                    [
                        jnp.where(resets_ref[g * steps + token] == 0, 1.0, 0.0)
                        for g in range(segments)
                    ],
                    blocks,
                )
                states = [state * hold for state in states]
            gate = wide[at, :]
            sums = [skip * gate, None]
            for n in range(modes):
                states[n] = states[n] * decay[n] + gate
                term = gain[n] * states[n]
                sums[n % 2] = term if sums[n % 2] is None else sums[n % 2] + term
            local_ref[at, :] = sums[0] + sums[1]
        return tuple(states)

    def some_tokens(step, states):
        return lax.cond(
            busy_ref[step] == 0,
            lambda held: tokens(step, held, False),
            lambda held: tokens(step, held, True),
            states,
        )

    zero = jnp.zeros((sub, LANES), jnp.float32)
    states = lax.fori_loop(0, steps // GROUP, some_tokens, (zero,) * modes)
    for n in range(modes):
        by_mode[0, n * sub : (n + 1) * sub, :] = states[n]
    open_shard = clear_ref[0]
    for g in range(1, segments):
        open_shard = open_shard * clear_ref[g]
    for j in range(blocks):
        lanes = slice(j * LANES, (j + 1) * LANES)
        entering = jnp.zeros((modes, LANES), jnp.float32)
        for g in range(segments):
            base_ref[g, :, lanes] = entering
            ended = by_mode[0, pl.ds(g * blocks + j, modes, stride=sub), :]
            entering = ended + across_ref[:, lanes] * clear_ref[g] * entering
        ended_ref[:, chunk * width + j * LANES : chunk * width + (j + 1) * LANES] = (
            entering.astype(ended_ref.dtype)
        )
    ended_ref[:, (chunk + 1) * width :] = jnp.full(
        (modes, LANES), open_shard, jnp.float32
    ).astype(ended_ref.dtype)


def whole_block(shape):
    return pl.BlockSpec(shape, lambda g: (0,) * len(shape))


def scan_shard(
    chunk, width, segments, slots, resets, busy, clear, slabs, edges, before, tables, earlier
):
    count, rows, _ = slabs.shape
    length = resets.shape[0]
    modes, channels = tables[1].shape
    blocks = width // LANES
    sub = segments * blocks
    outs = [
        jax.ShapeDtypeStruct((length, channels), jnp.bfloat16),
        jax.ShapeDtypeStruct((length * channels // LANES, LANES), jnp.float32),
        jax.ShapeDtypeStruct((segments, modes, channels), jnp.float32),
        jax.ShapeDtypeStruct((modes, (chunk + 1) * width + LANES), jnp.bfloat16),
    ]
    shared = [*earlier[3:], *earlier[:3]]
    first = 7 + len(tables) + 1
    return pl.pallas_call(
        functools.partial(scan_body, chunk, segments, len(shared)),
        grid=(1,),
        in_specs=[SMEM] * 4 + [ANY] * 3
        + [columns_of(table, chunk, width) for table in tables]
        + [whole_block(value.shape) for value in shared[:1]]
        + [ANY] * len(shared[1:]),
        out_specs=[
            columns_of(outs[0], chunk, width),
            pl.BlockSpec((length * blocks, LANES), lambda g: (chunk, 0)),
            columns_of(outs[2], chunk, width),
            whole_block(outs[3].shape),
        ],
        out_shape=outs,
        input_output_aliases={first + i: i for i in range(len(shared[1:]))},
        scratch_shapes=[
            pltpu.VMEM((count, rows, width), jnp.bfloat16),
            pltpu.VMEM((count + 1, edges.shape[1], width), jnp.bfloat16),
            pltpu.VMEM((length * blocks + sub, LANES), jnp.float32),
            pltpu.VMEM((3, (modes + 1) * sub, LANES), jnp.float32),
            pltpu.SemaphoreType.DMA((2 * count + 1,)),
        ],
        compiler_params=PARAMS,
        cost_estimate=pl.CostEstimate(
            flops=100 * length * width, bytes_accessed=10 * length * width, transcendentals=0
        ),
        name="scan_shard",
    )(slots, resets, busy, clear, slabs, edges, before, *tables, *shared)


def carry_body(segments, count, *refs):
    limit_ref, clear_ref = refs[:2]
    end_refs = refs[2 : 2 + count]
    through_ref, across_ref, decay_ref, gain_ref = refs[2 + count : 6 + count]
    base_ref, front_ref, local_ref = refs[6 + count : 9 + count]
    out_ref, by_mode, carried = refs[-3:]
    modes, width = decay_ref.shape
    length = front_ref.shape[0]
    blocks = width // LANES
    sub = segments * blocks
    steps = length // segments
    part = min(64, steps)
    for j in range(blocks):
        lanes = slice(j * LANES, (j + 1) * LANES)
        here = pl.ds(pl.multiple_of(pl.program_id(0) * width + j * LANES, LANES), LANES)
        entering = jnp.zeros((modes, LANES), jnp.float32)
        for ref in reversed(end_refs):
            is_open = ref[:, ref.shape[1] - LANES :].astype(jnp.float32)
            entering = ref[:, here].astype(jnp.float32) + (
                through_ref[:, lanes] * is_open * entering
            )
        for g in range(segments):
            at = pl.ds(g * blocks + j, modes, stride=sub)
            by_mode[0, at, :] = decay_ref[:, lanes]
            by_mode[1, at, :] = gain_ref[:, lanes] * (base_ref[g, :, lanes] + entering)
            entering = entering * across_ref[:, lanes] * clear_ref[g]
    decay = [mode_rows(by_mode, 0, n, sub) for n in range(modes)]
    limit = spread([jnp.full((sub, LANES), limit_ref[g]) for g in range(segments)], blocks)

    def some_tokens(step, states):
        states = list(states)
        for u in range(GROUP):
            token = step * GROUP + u
            at = pl.ds(pl.multiple_of(token * sub, sub), sub)
            sums = [None] * 4
            for n in range(modes):
                states[n] = states[n] * decay[n]
                sums[n % 4] = states[n] if sums[n % 4] is None else sums[n % 4] + states[n]
            added = (sums[0] + sums[1]) + (sums[2] + sums[3])
            carried[at, :] = local_ref[at, :] + jnp.where(token < limit, added, 0.0)
        return tuple(states)

    lax.fori_loop(
        0,
        steps // GROUP,
        some_tokens,
        tuple(mode_rows(by_mode, 1, n, sub) for n in range(modes)),
    )

    def finish(step, carry):
        first = step * part
        g, t = first // steps, first % steps
        rows = pl.ds(pl.multiple_of(first, part), part)
        for j in range(blocks):
            lanes = slice(j * LANES, (j + 1) * LANES)
            total = carried[pl.ds(t * sub + (g * blocks + j), part, stride=sub), :]
            out_ref[rows, lanes] = (front_ref[rows, lanes].astype(jnp.float32) * total).astype(
                out_ref.dtype
            )
        return carry

    lax.fori_loop(0, length // part, finish, 0)


def carry_shard(width, segments, limit, clear, ends, tables, base, front, local):
    length, channels = front.shape
    modes = tables[0].shape[0]
    blocks = width // LANES
    sub = segments * blocks
    specs = [SMEM, SMEM]
    specs += [whole_block(value.shape) for value in ends]
    specs += [pl.BlockSpec((modes, width), lambda g: (0, g)) for table in tables]
    specs.append(pl.BlockSpec((segments, modes, width), lambda g: (0, 0, g)))
    specs.append(pl.BlockSpec((length, width), lambda g: (0, g)))
    specs.append(pl.BlockSpec((length * blocks, LANES), lambda g: (g, 0)))
    return pl.pallas_call(
        functools.partial(carry_body, segments, len(ends)),
        grid=(channels // width,),
        in_specs=specs,
        out_specs=pl.BlockSpec((length, width), lambda g: (0, g)),
        out_shape=jax.ShapeDtypeStruct((length, channels), jnp.bfloat16),
        scratch_shapes=[
            pltpu.VMEM((2, (modes + 1) * sub, LANES), jnp.float32),
            pltpu.VMEM((length * blocks + sub, LANES), jnp.float32),
        ],
        compiler_params=pltpu.CompilerParams(vmem_limit_bytes=52 * 1024 * 1024),
        cost_estimate=pl.CostEstimate(
            flops=40 * length * channels, bytes_accessed=8 * length * channels, transcendentals=0
        ),
        name="carry_shard",
    )(limit, clear, *ends, *tables, base, front, local)


def on_device(arrived, landing, resets, short_taps, decay_rate, residues, skip_gain):
    shards, chans = lax.axis_size("seq"), lax.axis_size("chan")
    chan = lax.axis_index("chan")
    per_device = shards // chans
    length = resets.shape[0]
    channels = short_taps.shape[2]
    reach = short_taps.shape[1] - 1
    width = channels // CHUNKS
    segments = max(1, SUBLANES * LANES // width)

    def passed_along(value, by):
        return lax.ppermute(value, "seq", [(i, i + by) for i in range(shards - by)])

    place = chan.astype(jnp.int32)[None]
    slots = landing[0]
    final = jnp.argmax(slots == shards - 1)
    marks = resets.reshape(segments, -1)
    steps = marks.shape[1]
    limit = jnp.min(
        jnp.where(marks != 0, lax.broadcasted_iota(jnp.int32, marks.shape, 1), steps), axis=1
    )
    clear = (limit == steps).astype(jnp.float32)
    busy = jnp.sum(marks.reshape(segments, -1, GROUP), axis=(0, 2))
    decay = jnp.exp(-decay_rate)
    through = jnp.exp(-decay_rate * length)
    across = jnp.exp(-decay_rate * steps)
    gain = residues * jnp.sqrt(-jnp.expm1(-2.0 * decay_rate))
    skip = skip_gain[None]

    def across_plane(parts):
        return [
            lax.ppermute(part, "chan", [(c, c ^ d) for c in range(chans)])
            for d, part in enumerate(parts, start=1)
        ]

    def along_column(value):
        return lax.all_to_all(value, "seq", split_axis=0, concat_axis=0, tiled=True)

    own, *parts = cut_edges(place, arrived, per_device, reach, channels, chans)
    parts = [own, *across_plane(parts)]
    cuts = [cut_blocks(0, width, chans, place, arrived, [own])]
    edges = along_column(by_shard(place, parts, cuts[0]))
    last = lax.dynamic_index_in_dim(edges, final, axis=0, keepdims=False)
    before = passed_along(last, 1)

    scanned, ended = [], []
    for chunk in range(CHUNKS):
        blocks = across_plane(cuts[chunk])
        ready = []
        if 0 < chunk < CHUNKS - 1:
            cuts.append(cut_blocks(chunk + 1, width, chans, place, arrived, [sent]))
            ready = [*ready, cuts[-1][0]]
        sent = slab_fronts(
            chunk, width, place, arrived, blocks, short_taps, per_device, ready
        )
        if chunk == CHUNKS - 1:
            sent = in_place(sent, before)
        if chunk == 0:
            cuts.append(cut_blocks(1, width, chans, place, arrived, [sent]))
        scanned = scan_shard(
            chunk,
            width,
            segments,
            slots,
            resets,
            busy,
            clear,
            along_column(sent),
            edges,
            before,
            (short_taps, decay, gain, skip, across),
            scanned,
        )
        ended.append(scanned[3])
    front, local, base, _ = scanned
    ends = [passed_along(ended[-1], d) for d in range(1, shards)]
    return carry_shard(
        width, segments, limit, clear, ends, (through, across, decay, gain), base, front, local
    )


def solution(mesh):
    in_specs = (
        P(None, ("seq", "chan"), None),
        P("seq", None),
        P("seq"),
        P(None, None, "chan"),
        P(None, "chan"),
        P(None, "chan"),
        P("chan"),
    )
    out_specs = P("seq", "chan")
    return jax.shard_map(
        on_device, mesh=mesh, in_specs=in_specs, out_specs=out_specs, check_vma=False
    )
```

```python
import functools

import jax
import jax.numpy as jnp
from jax import lax
from jax.experimental import pallas as pl
from jax.experimental.pallas import tpu as pltpu
from jax.sharding import PartitionSpec as P

LANES = 128
SUBLANES = 8
GROUP = 32
CHUNKS = 4
VMEM_BYTES = 50 * 1024 * 1024

SMEM = pl.BlockSpec(memory_space=pltpu.SMEM)
VMEM = pl.BlockSpec(memory_space=pltpu.VMEM)
ANY = pl.BlockSpec(memory_space=pl.ANY)
PARAMS = pltpu.CompilerParams(vmem_limit_bytes=VMEM_BYTES)


def columns_of(table, chunk, width):
    lead = table.shape[:-1]
    return pl.BlockSpec((*lead, width), lambda g: (0,) * len(lead) + (chunk,))


def column_start(place_ref, d, chunk, width):
    return pl.multiple_of(((place_ref[0] ^ d) * CHUNKS + chunk) * width, LANES)


def cut_blocks(chunk, width, chans, place, arrived, later):

    def body(place_ref, arrived_ref, *refs):
        outs, sems = refs[len(later) : -1], refs[-1]
        copies = []
        for d, out in enumerate(outs, start=1):
            start = column_start(place_ref, d, chunk, width)
            copies.append(
                pltpu.make_async_copy(
                    arrived_ref.at[:, :, pl.ds(start, width)], out, sems.at[d - 1]
                )
            )
        for copy in copies:
            copy.start()
        for copy in copies:
            copy.wait()

    shape = jax.ShapeDtypeStruct((*arrived.shape[:2], width), arrived.dtype)
    return pl.pallas_call(
        body,
        in_specs=[SMEM, ANY] + [ANY] * len(later),
        out_specs=[VMEM] * (chans - 1),
        out_shape=[shape] * (chans - 1),
        scratch_shapes=[pltpu.SemaphoreType.DMA((chans - 1,))],
        compiler_params=PARAMS,
        name="cut_blocks",
    )(place, arrived, *later)


def shift_window(rows, start, count):
    return lax.slice_in_dim(rows, start, start + count, axis=0)


def cut_edges(place, arrived, per_device, reach, channels, chans):
    slab = arrived.shape[1] // per_device

    def body(place_ref, arrived_ref, *refs):
        outs, (tails, heads, sems) = refs[:chans], refs[chans:]
        copies = []
        for d in range(chans):
            start = pl.multiple_of((place_ref[0] ^ d) * channels, LANES)
            here = pl.ds(start, channels)
            for i in range(per_device):
                at = len(copies)
                copies.append(
                    pltpu.make_async_copy(
                        arrived_ref.at[:, pl.ds((i + 1) * slab - 16, 16), here],
                        tails.at[d, i],
                        sems.at[at],
                    )
                )
                copies.append(
                    pltpu.make_async_copy(
                        arrived_ref.at[2, pl.ds(i * slab, 16), here],
                        heads.at[d, i],
                        sems.at[at + 1],
                    )
                )
        for copy in copies:
            copy.start()
        for copy in copies:
            copy.wait()

        for d in range(chans):

            def one_block(block, carry, d=d):
                lanes = pl.ds(pl.multiple_of(block * LANES, LANES), LANES)
                for i in range(per_device):
                    parts = [
                        tails[d, i, k, :, lanes].astype(jnp.float32)[16 - reach :] for k in range(3)
                    ]
                    parts.append(heads[d, i, :, lanes].astype(jnp.float32)[:reach])
                    outs[d][i, :, lanes] = jnp.concatenate(parts, axis=0).astype(arrived.dtype)
                return carry

            lax.fori_loop(0, channels // LANES, one_block, 0)

    shape = jax.ShapeDtypeStruct((per_device, 4 * reach, channels), arrived.dtype)
    return pl.pallas_call(
        body,
        in_specs=[SMEM, ANY],
        out_specs=[VMEM] * chans,
        out_shape=[shape] * chans,
        scratch_shapes=[
            pltpu.VMEM((chans, per_device, 3, 16, channels), arrived.dtype),
            pltpu.VMEM((chans, per_device, 16, channels), arrived.dtype),
            pltpu.SemaphoreType.DMA((2 * chans * per_device,)),
        ],
        compiler_params=PARAMS,
        name="cut_edges",
    )(place, arrived)


def by_shard(place, parts, later):
    count = len(parts)
    per_device, rows, channels = parts[0].shape

    def body(place_ref, *refs):
        part_refs, (out_ref, sems) = refs[:count], refs[-2:]
        copies = [
            pltpu.make_async_copy(
                part_refs[d],
                out_ref.at[pl.ds((place_ref[0] ^ d) * per_device, per_device)],
                sems.at[d],
            )
            for d in range(count)
        ]
        for copy in copies:
            copy.start()
        for copy in copies:
            copy.wait()

    return pl.pallas_call(
        body,
        in_specs=[SMEM] + [ANY] * (count + len(later)),
        out_specs=VMEM,
        out_shape=jax.ShapeDtypeStruct((count * per_device, rows, channels), parts[0].dtype),
        scratch_shapes=[pltpu.SemaphoreType.DMA((count,))],
        compiler_params=PARAMS,
        name="by_shard",
    )(place, *parts, *later)


def in_place(value, later):
    def body(value_ref, later_ref, out_ref):
        pass

    return pl.pallas_call(
        body,
        in_specs=[ANY, ANY],
        out_specs=ANY,
        out_shape=jax.ShapeDtypeStruct(value.shape, value.dtype),
        input_output_aliases={0: 0},
        compiler_params=PARAMS,
        name="in_place",
    )(value, later)


def front_body(chunk, count, place_ref, arrived_ref, *refs):
    block_refs = refs[: count - 1]
    taps_ref, out_ref, held, padded, sems = refs[-5:]
    shards, _, width = out_ref.shape
    per_device = shards // count
    slab = held.shape[2] // per_device
    taps = taps_ref.shape[1]
    reach = taps - 1
    blocks = width // LANES
    row_ids = lax.broadcasted_iota(jnp.int32, (slab, LANES), 0)
    sources = [arrived_ref.at[:, :, pl.ds(column_start(place_ref, 0, chunk, width), width)]]
    sources += block_refs
    copies = [pltpu.make_async_copy(sources[d], held.at[d], sems.at[d]) for d in range(count)]
    for copy in copies:
        copy.start()
    for k in range(3):
        padded[k, :8, :] = jnp.zeros((8, LANES), jnp.float32)
    for d in range(count):
        copies[d].wait()

        def one_block(step, carry, d=d):
            i, block = step // blocks, step % blocks
            lanes = pl.ds(pl.multiple_of(block * LANES, LANES), LANES)
            own = pl.ds(pl.multiple_of(i * slab, slab), slab)
            shard = (place_ref[0] ^ d) * per_device + i

            def conv(k):
                rows = held[d, k, own, lanes].astype(jnp.float32)
                padded[k, 8:, :] = rows
                total = taps_ref[k, 0:1, lanes] * rows
                for j in range(1, taps):
                    total = total + taps_ref[k, j : j + 1, lanes] * padded[k, 8 - j : 8 - j + slab, :]
                return total

            front = conv(0)
            key = conv(1)
            value = conv(2)
            gate = jnp.where(row_ids < reach, key, key * value)
            out_ref[shard, :slab, lanes] = front.astype(out_ref.dtype)
            out_ref[shard, slab:, lanes] = gate.astype(out_ref.dtype)
            return carry

        lax.fori_loop(0, per_device * blocks, one_block, 0, unroll=2)


def slab_fronts(chunk, width, place, arrived, blocks, taps, per_device, after):
    count = len(blocks) + 1
    rows = arrived.shape[1]
    shape = (count * per_device, 2 * (rows // per_device), width)
    return pl.pallas_call(
        functools.partial(front_body, chunk, count),
        grid=(1,),
        in_specs=[SMEM] + [ANY] * (count + len(after)) + [columns_of(taps, chunk, width)],
        out_specs=pl.BlockSpec(shape, lambda g: (0, 0, 0)),
        out_shape=jax.ShapeDtypeStruct(shape, arrived.dtype),
        scratch_shapes=[
            pltpu.VMEM((count, 3, rows, width), arrived.dtype),
            pltpu.VMEM((3, rows // per_device + 8, LANES), jnp.float32),
            pltpu.SemaphoreType.DMA((count,)),
        ],
        compiler_params=PARAMS,
        cost_estimate=pl.CostEstimate(
            flops=60 * count * rows * width,
            bytes_accessed=10 * count * rows * width,
            transcendentals=0,
        ),
        name="slab_fronts",
    )(place, arrived, *blocks, *after, taps)


def spread(values, blocks):
    if len(values) == 1:
        return values[0]
    ids = lax.broadcasted_iota(jnp.int32, (len(values) * blocks, LANES), 0)
    out = jnp.full(ids.shape, values[-1])
    for g in range(len(values) - 2, -1, -1):
        out = jnp.where(ids < (g + 1) * blocks, values[g], out)
    return out


def mode_rows(ref, table, n, sub):
    return ref[table, n * sub : (n + 1) * sub, :]


def scan_body(chunk, segments, shared, *refs):
    slots_ref, resets_ref, busy_ref, clear_ref, slab_ref, edge_ref, before_ref = refs[:7]
    taps_ref, decay_ref, gain_ref, skip_ref, across_ref = refs[7:12]
    earlier_refs = refs[12 : 12 + (shared > 0)]
    front_ref, local_ref, base_ref, ended_ref = refs[12 + shared : 16 + shared]
    slabs, edges, wide, by_mode, sems = refs[16 + shared :]
    count, rows, width = slabs.shape
    taps = taps_ref.shape[1]
    reach = taps - 1
    slab = rows // 2
    modes = decay_ref.shape[0]
    blocks = width // LANES
    sub = segments * blocks
    steps = count * slab // segments

    here = pl.ds(chunk * width, width)
    copies = [pltpu.make_async_copy(before_ref.at[:, here], edges.at[0], sems.at[2 * count])]
    for m in range(count):
        slot = slots_ref[m]
        copies.append(pltpu.make_async_copy(slab_ref.at[m], slabs.at[slot], sems.at[m]))
        copies.append(
            pltpu.make_async_copy(
                edge_ref.at[m, :, here], edges.at[slot + 1], sems.at[count + m]
            )
        )
    for copy in copies:
        copy.start()
    for g in range(segments):
        for j in range(blocks):
            lanes = slice(j * LANES, (j + 1) * LANES)
            at = g * blocks + j
            by_mode[0, pl.ds(at, modes, stride=sub), :] = decay_ref[:, lanes]
            by_mode[1, pl.ds(at, modes, stride=sub), :] = gain_ref[:, lanes]
            by_mode[2, at : at + 1, :] = skip_ref[:, lanes]
    for ref in earlier_refs:
        ended_ref[:, : chunk * width] = ref[:, : chunk * width]
    for copy in copies:
        copy.wait()

    row_ids = lax.broadcasted_iota(jnp.int32, (slab, LANES), 0)
    blank = jnp.zeros((16 - reach, LANES), jnp.float32)

    def one_slot(slot, carry):
        first = slot * slab
        g, t = first // steps, first % steps
        for j in range(blocks):
            lanes = slice(j * LANES, (j + 1) * LANES)
            edge = edges[slot, :, lanes].astype(jnp.float32)
            own = edges[slot + 1, :, lanes].astype(jnp.float32)

            def from_rows(k, rows, least):
                total = jnp.zeros((8, LANES), jnp.float32)
                for tap in range(least, taps):
                    total = total + taps_ref[k, tap : tap + 1, lanes] * shift_window(
                        rows, reach - tap, 8
                    )
                return total

            def tail(k):
                return edge[k * reach : (k + 1) * reach]

            add_front = from_rows(0, jnp.concatenate([tail(0), blank], axis=0), 1)
            add_key = from_rows(1, jnp.concatenate([tail(1), blank], axis=0), 1)
            value = from_rows(
                2, jnp.concatenate([tail(2), own[3 * reach :], blank[reach:]], axis=0), 0
            )
            starts = row_ids[:8] < reach
            front = slabs[slot, :slab, lanes].astype(jnp.float32)
            gate = slabs[slot, slab:, lanes].astype(jnp.float32)
            front_start = jnp.where(starts, front[:8] + add_front, front[:8])
            gate_start = ((gate[:8] + add_key) * value).astype(jnp.bfloat16)
            gate_start = jnp.where(starts, gate_start.astype(jnp.float32), gate[:8])
            front = jnp.concatenate([front_start, front[8:]], axis=0)
            gate = jnp.concatenate([gate_start, gate[8:]], axis=0)
            base = pl.multiple_of(first, slab)
            front_ref[pl.ds(base, slab), lanes] = front.astype(front_ref.dtype)
            wide[pl.ds(t * sub + (g * blocks + j), slab, stride=sub), :] = gate

        return carry

    lax.fori_loop(0, count, one_slot, 0)

    decay = [mode_rows(by_mode, 0, n, sub) for n in range(modes)]
    gain = [mode_rows(by_mode, 1, n, sub) for n in range(modes)]
    skip = by_mode[2, 0:sub, :]

    def tokens(step, states, with_resets):
        states = list(states)
        for u in range(GROUP):
            token = step * GROUP + u
            at = pl.ds(pl.multiple_of(token * sub, sub), sub)
            if with_resets:
                hold = spread(
                    [
                        jnp.where(resets_ref[g * steps + token] == 0, 1.0, 0.0)
                        for g in range(segments)
                    ],
                    blocks,
                )
                states = [state * hold for state in states]
            gate = wide[at, :]
            sums = [skip * gate, None]
            for n in range(modes):
                states[n] = states[n] * decay[n] + gate
                term = gain[n] * states[n]
                sums[n % 2] = term if sums[n % 2] is None else sums[n % 2] + term
            local_ref[at, :] = sums[0] + sums[1]
        return tuple(states)

    def some_tokens(step, states):
        return lax.cond(
            busy_ref[step] == 0,
            lambda held: tokens(step, held, False),
            lambda held: tokens(step, held, True),
            states,
        )

    zero = jnp.zeros((sub, LANES), jnp.float32)
    states = lax.fori_loop(0, steps // GROUP, some_tokens, (zero,) * modes)
    for n in range(modes):
        by_mode[0, n * sub : (n + 1) * sub, :] = states[n]
    open_shard = clear_ref[0]
    for g in range(1, segments):
        open_shard = open_shard * clear_ref[g]
    for j in range(blocks):
        lanes = slice(j * LANES, (j + 1) * LANES)
        entering = jnp.zeros((modes, LANES), jnp.float32)
        for g in range(segments):
            base_ref[g, :, lanes] = entering
            ended = by_mode[0, pl.ds(g * blocks + j, modes, stride=sub), :]
            entering = ended + across_ref[:, lanes] * clear_ref[g] * entering
        ended_ref[:, chunk * width + j * LANES : chunk * width + (j + 1) * LANES] = (
            entering.astype(ended_ref.dtype)
        )
    ended_ref[:, (chunk + 1) * width :] = jnp.full(
        (modes, LANES), open_shard, jnp.float32
    ).astype(ended_ref.dtype)


def whole_block(shape):
    return pl.BlockSpec(shape, lambda g: (0,) * len(shape))


def scan_shard(
    chunk, width, segments, slots, resets, busy, clear, slabs, edges, before, tables, earlier
):
    count, rows, _ = slabs.shape
    length = resets.shape[0]
    modes, channels = tables[1].shape
    blocks = width // LANES
    sub = segments * blocks
    outs = [
        jax.ShapeDtypeStruct((length, channels), jnp.bfloat16),
        jax.ShapeDtypeStruct((length * channels // LANES, LANES), jnp.float32),
        jax.ShapeDtypeStruct((segments, modes, channels), jnp.float32),
        jax.ShapeDtypeStruct((modes, (chunk + 1) * width + LANES), jnp.bfloat16),
    ]
    shared = [*earlier[3:], *earlier[:3]]
    first = 7 + len(tables) + 1
    return pl.pallas_call(
        functools.partial(scan_body, chunk, segments, len(shared)),
        grid=(1,),
        in_specs=[SMEM] * 4 + [ANY] * 3
        + [columns_of(table, chunk, width) for table in tables]
        + [whole_block(value.shape) for value in shared[:1]]
        + [ANY] * len(shared[1:]),
        out_specs=[
            columns_of(outs[0], chunk, width),
            pl.BlockSpec((length * blocks, LANES), lambda g: (chunk, 0)),
            columns_of(outs[2], chunk, width),
            whole_block(outs[3].shape),
        ],
        out_shape=outs,
        input_output_aliases={first + i: i for i in range(len(shared[1:]))},
        scratch_shapes=[
            pltpu.VMEM((count, rows, width), jnp.bfloat16),
            pltpu.VMEM((count + 1, edges.shape[1], width), jnp.bfloat16),
            pltpu.VMEM((length * blocks + sub, LANES), jnp.float32),
            pltpu.VMEM((3, (modes + 1) * sub, LANES), jnp.float32),
            pltpu.SemaphoreType.DMA((2 * count + 1,)),
        ],
        compiler_params=PARAMS,
        cost_estimate=pl.CostEstimate(
            flops=100 * length * width, bytes_accessed=10 * length * width, transcendentals=0
        ),
        name="scan_shard",
    )(slots, resets, busy, clear, slabs, edges, before, *tables, *shared)


def carry_body(segments, count, *refs):
    limit_ref, clear_ref = refs[:2]
    end_refs = refs[2 : 2 + count]
    through_ref, across_ref, decay_ref, gain_ref = refs[2 + count : 6 + count]
    base_ref, front_ref, local_ref = refs[6 + count : 9 + count]
    out_ref, by_mode, carried = refs[-3:]
    modes, width = decay_ref.shape
    length = front_ref.shape[0]
    blocks = width // LANES
    sub = segments * blocks
    steps = length // segments
    part = min(64, steps)
    for j in range(blocks):
        lanes = slice(j * LANES, (j + 1) * LANES)
        here = pl.ds(pl.multiple_of(pl.program_id(0) * width + j * LANES, LANES), LANES)
        entering = jnp.zeros((modes, LANES), jnp.float32)
        for ref in reversed(end_refs):
            is_open = ref[:, ref.shape[1] - LANES :].astype(jnp.float32)
            entering = ref[:, here].astype(jnp.float32) + (
                through_ref[:, lanes] * is_open * entering
            )
        for g in range(segments):
            at = pl.ds(g * blocks + j, modes, stride=sub)
            by_mode[0, at, :] = decay_ref[:, lanes]
            by_mode[1, at, :] = gain_ref[:, lanes] * (base_ref[g, :, lanes] + entering)
            entering = entering * across_ref[:, lanes] * clear_ref[g]
    decay = [mode_rows(by_mode, 0, n, sub) for n in range(modes)]
    limit = spread([jnp.full((sub, LANES), limit_ref[g]) for g in range(segments)], blocks)

    def some_tokens(step, states):
        states = list(states)
        for u in range(GROUP):
            token = step * GROUP + u
            at = pl.ds(pl.multiple_of(token * sub, sub), sub)
            sums = [None] * 4
            for n in range(modes):
                states[n] = states[n] * decay[n]
                sums[n % 4] = states[n] if sums[n % 4] is None else sums[n % 4] + states[n]
            added = (sums[0] + sums[1]) + (sums[2] + sums[3])
            carried[at, :] = local_ref[at, :] + jnp.where(token < limit, added, 0.0)
        return tuple(states)

    lax.fori_loop(
        0,
        steps // GROUP,
        some_tokens,
        tuple(mode_rows(by_mode, 1, n, sub) for n in range(modes)),
    )

    def finish(step, carry):
        first = step * part
        g, t = first // steps, first % steps
        rows = pl.ds(pl.multiple_of(first, part), part)
        for j in range(blocks):
            lanes = slice(j * LANES, (j + 1) * LANES)
            total = carried[pl.ds(t * sub + (g * blocks + j), part, stride=sub), :]
            out_ref[rows, lanes] = (front_ref[rows, lanes].astype(jnp.float32) * total).astype(
                out_ref.dtype
            )
        return carry

    lax.fori_loop(0, length // part, finish, 0)


def carry_shard(width, segments, limit, clear, ends, tables, base, front, local):
    length, channels = front.shape
    modes = tables[0].shape[0]
    blocks = width // LANES
    sub = segments * blocks
    specs = [SMEM, SMEM]
    specs += [whole_block(value.shape) for value in ends]
    specs += [pl.BlockSpec((modes, width), lambda g: (0, g)) for table in tables]
    specs.append(pl.BlockSpec((segments, modes, width), lambda g: (0, 0, g)))
    specs.append(pl.BlockSpec((length, width), lambda g: (0, g)))
    specs.append(pl.BlockSpec((length * blocks, LANES), lambda g: (g, 0)))
    return pl.pallas_call(
        functools.partial(carry_body, segments, len(ends)),
        grid=(channels // width,),
        in_specs=specs,
        out_specs=pl.BlockSpec((length, width), lambda g: (0, g)),
        out_shape=jax.ShapeDtypeStruct((length, channels), jnp.bfloat16),
        scratch_shapes=[
            pltpu.VMEM((2, (modes + 1) * sub, LANES), jnp.float32),
            pltpu.VMEM((length * blocks + sub, LANES), jnp.float32),
        ],
        compiler_params=pltpu.CompilerParams(vmem_limit_bytes=52 * 1024 * 1024),
        cost_estimate=pl.CostEstimate(
            flops=40 * length * channels, bytes_accessed=8 * length * channels, transcendentals=0
        ),
        name="carry_shard",
    )(limit, clear, *ends, *tables, base, front, local)


def on_device(arrived, landing, resets, short_taps, decay_rate, residues, skip_gain):
    shards, chans = lax.axis_size("seq"), lax.axis_size("chan")
    chan = lax.axis_index("chan")
    per_device = shards // chans
    length = resets.shape[0]
    channels = short_taps.shape[2]
    reach = short_taps.shape[1] - 1
    width = channels // CHUNKS
    segments = max(1, SUBLANES * LANES // width)

    def passed_along(value, by):
        return lax.ppermute(value, "seq", [(i, i + by) for i in range(shards - by)])

    place = chan.astype(jnp.int32)[None]
    slots = landing[0]
    final = jnp.argmax(slots == shards - 1)
    marks = resets.reshape(segments, -1)
    steps = marks.shape[1]
    limit = jnp.min(
        jnp.where(marks != 0, lax.broadcasted_iota(jnp.int32, marks.shape, 1), steps), axis=1
    )
    clear = (limit == steps).astype(jnp.float32)
    busy = jnp.sum(marks.reshape(segments, -1, GROUP), axis=(0, 2))
    decay = jnp.exp(-decay_rate)
    through = jnp.exp(-decay_rate * length)
    across = jnp.exp(-decay_rate * steps)
    gain = residues * jnp.sqrt(-jnp.expm1(-2.0 * decay_rate))
    skip = skip_gain[None]

    def across_plane(parts):
        return [
            lax.ppermute(part, "chan", [(c, c ^ d) for c in range(chans)])
            for d, part in enumerate(parts, start=1)
        ]

    def along_column(value):
        return lax.all_to_all(value, "seq", split_axis=0, concat_axis=0, tiled=True)

    own, *parts = cut_edges(place, arrived, per_device, reach, channels, chans)
    parts = [own, *across_plane(parts)]
    cuts = [cut_blocks(0, width, chans, place, arrived, [own])]
    edges = along_column(by_shard(place, parts, cuts[0]))
    last = lax.dynamic_index_in_dim(edges, final, axis=0, keepdims=False)
    before = passed_along(last, 1)

    scanned, ended = [], []
    for chunk in range(CHUNKS):
        blocks = across_plane(cuts[chunk])
        ready = []
        if 0 < chunk < CHUNKS - 1:
            cuts.append(cut_blocks(chunk + 1, width, chans, place, arrived, [sent]))
            ready = [*ready, cuts[-1][0]]
        sent = slab_fronts(
            chunk, width, place, arrived, blocks, short_taps, per_device, ready
        )
        if chunk == CHUNKS - 1:
            sent = in_place(sent, before)
        if chunk == 0:
            cuts.append(cut_blocks(1, width, chans, place, arrived, [sent]))
        scanned = scan_shard(
            chunk,
            width,
            segments,
            slots,
            resets,
            busy,
            clear,
            along_column(sent),
            edges,
            before,
            (short_taps, decay, gain, skip, across),
            scanned,
        )
        ended.append(scanned[3])
    front, local, base, _ = scanned
    ends = [passed_along(ended[-1], d) for d in range(1, shards)]
    return carry_shard(
        width, segments, limit, clear, ends, (through, across, decay, gain), base, front, local
    )


def solution(mesh):
    in_specs = (
        P(None, ("seq", "chan"), None),
        P("seq", None),
        P("seq"),
        P(None, None, "chan"),
        P(None, "chan"),
        P(None, "chan"),
        P("chan"),
    )
    out_specs = P("seq", "chan")
    return jax.shard_map(
        on_device, mesh=mesh, in_specs=in_specs, out_specs=out_specs, check_vma=False
    )
```
